32 devices in a mesh: rx: 8 (over z, y), ry: 4 (over x, core).
Axes of the slice: x: 2, y: 2, z: 4, core: 2. Of those that a mesh axis runs over, the one named last changes fastest.
Arguments:
- matrix: float32 [131072, 256], P(('rx', 'ry')), may hold values from -6 to 6
- signs: int32 [131072], P(('rx', 'ry')), may hold values from -1 to 1, as said below
- indices: int32 [8192], P(('rx', 'ry')), may hold values from 0 to 4095, as said below
- counts: int32 [32], P(('rx', 'ry')), may hold values from 64 to 256, as said below
Outputs:
- sketch: float32 [8192, 256], P(('rx', 'ry'))
- gram_blocks: float32 [4, 128, 128], P('ry')
The draws below stay inside these ranges and needn't reach their ends.
Inputs may be any that keep to these rules, and one draw needn't show every extreme that they name: `signs`: each entry is -1 or 1. `indices`: local row numbers; repeats allowed; entries of dead slots are ignored. `counts`: some device has all 256 slots live.
All inputs are finite; a program needn't handle non-finite values.
Results may differ from the reference program's by a relative error of at most 0.00011.
Values sent between devices are 32-bit elements; how exact they have to be, the bound alone decides.
No kernel may reach another device: no remote copies, remote signals or barrier semaphores. Data moves between devices by JAX's collectives and lax.ppermute only.
A program may use at most 64 MiB of HBM per device.

```python
import jax
import jax.numpy as jnp
from jax import lax

PANEL = 128
COLS = 256
BLK = 128
ROWS_DEV = 4096
CAP = 256
ROWS = 131072
SLOTS = 8192
N_RX = 8
N_RY = 4


def draw_signs(key, part):
    key = jax.random.fold_in(key, 11)
    return (2 * jax.random.randint(key, (ROWS,), 0, 2) - 1).astype(jnp.int32)


def draw_indices(key, part):
    key = jax.random.fold_in(key, 12)
    return jax.random.randint(key, (SLOTS,), 0, ROWS_DEV).astype(jnp.int32)


def draw_counts(key, part):
    key = jax.random.fold_in(key, 13)
    first, second = jax.random.split(key)
    values = jax.random.randint(first, (N_RX * N_RY,), CAP // 4, CAP + 1)
    fullest = jax.random.randint(second, (), 0, N_RX * N_RY)
    return values.at[fullest].set(CAP).astype(jnp.int32)


def levels(key, shape, cuts, least, largest):
    gain, own = 1.0, jax.random.fold_in(key, 6)
    for axis_at, shards_of in cuts:
        heights = jnp.exp(jax.random.uniform(jax.random.fold_in(own, axis_at), (shards_of,), jnp.float32, least / len(cuts), largest / len(cuts)))
        gain = gain * jnp.repeat(heights, shape[axis_at] // shards_of).reshape([-1 if axis == axis_at else 1 for axis in range(len(shape))])
    return gain


def normal_values(rng, dims, spread, limit, shards=(), kind=jnp.bfloat16):
    drawn = spread * jax.random.normal(rng, dims, jnp.float32)
    if shards:
        drawn = drawn * levels(rng, dims, shards, -0.22, 0.18)
    return jnp.clip(drawn, -limit, limit).astype(kind)


def setup_inputs(seed: int = 0) -> dict:
    seeds = jax.random.split(jax.random.key(seed), 5)
    return {
        "matrix": normal_values(seeds[0], (ROWS, COLS), 1.0, 6.0, ((0, 32),), jnp.float32),
        "signs": draw_signs(jax.random.fold_in(seeds[4], 71), 0),
        "indices": draw_indices(jax.random.fold_in(seeds[4], 71), 0),
        "counts": draw_counts(jax.random.fold_in(seeds[4], 71), 0),
    }


def hadamard(order):
    idx = jnp.arange(order, dtype=jnp.int32)
    both = jnp.bitwise_and(idx[:, None], idx[None, :])
    parity = jnp.zeros((order, order), jnp.int32)
    for shift in range(order.bit_length() - 1):
        parity = parity + jnp.bitwise_and(jnp.right_shift(both, shift), 1)
    return (1 - 2 * (parity % 2)).astype(jnp.float32)


def reference(matrix, signs, indices, counts):
    groups = N_RX * N_RY
    signed = matrix * signs[:, None].astype(jnp.float32)
    blocks = signed.reshape(ROWS // BLK, BLK, COLS)
    local = jnp.einsum("ij,bjc->bic", hadamard(BLK), blocks, precision=lax.Precision.HIGHEST)
    depth = groups.bit_length() - 1
    mixed = local.reshape((2,) * depth + (ROWS_DEV, COLS))
    for axis in range(depth):
        first = jnp.take(mixed, 0, axis)
        second = jnp.take(mixed, 1, axis)
        mixed = jnp.stack([first + second, first - second], axis)
    mixed = mixed.reshape(groups, ROWS_DEV, COLS) * (1.0 / (groups * BLK) ** 0.5)
    where_rows = indices.reshape(groups, CAP)
    live = jnp.arange(CAP, dtype=jnp.int32)[None, :] < counts[:, None]
    picked = jnp.take_along_axis(mixed, where_rows[:, :, None], axis=1)
    sketch = jnp.where(live[:, :, None], picked, jnp.float32(0.0)).reshape(groups * CAP, COLS)
    gram = jnp.dot(sketch.T, sketch, precision=lax.Precision.HIGHEST) * (1.0 / (groups * CAP))
    gram_blocks = gram.reshape(2, PANEL, 2, PANEL).transpose(0, 2, 1, 3).reshape(4, PANEL, PANEL)
    return sketch, gram_blocks
```

```python
import functools

import jax
import jax.numpy as jnp
from jax import lax
from jax.experimental import pallas as pl
from jax.experimental.pallas import tpu as pltpu
from jax.sharding import PartitionSpec as P

BLK = 128
MESH_AXES = ("rx", "ry")
GRANT = 12 * 2**20
WIDE = 46 * 2**20
AHEAD = 3
REST = 4


def swap(value, bits):
    size = lax.axis_size("rx") * lax.axis_size("ry")
    return lax.ppermute(value, MESH_AXES, [(i, i ^ bits) for i in range(size)])


def parity_sign(both):
    for shift in (4, 2, 1):
        both = jnp.bitwise_xor(both, jnp.right_shift(both, shift))
    return 1 - 2 * jnp.bitwise_and(both, 1)


def transform_kernel(full, chunks, me_ref, signs_ref, other_signs_ref, *refs):
    matrix_refs, table_ref, buffer_refs, sems = refs[:2], refs[2], refs[3:5], refs[5]
    rows, cols = table_ref.shape[0] // 2, table_ref.shape[1]
    step = rows // chunks

    def fetch(chunk):
        at = pl.ds(chunk * step, step)
        return [
            pltpu.make_async_copy(matrix_ref.at[at, :], buffer_ref.at[at, :], sems.at[chunk, which])
            for which, (matrix_ref, buffer_ref) in enumerate(zip(matrix_refs, buffer_refs))
        ]

    for chunk in range(AHEAD):
        for copy in fetch(chunk):
            copy.start()
    down = lax.broadcasted_iota(jnp.int32, (BLK, BLK), 0)
    across = lax.broadcasted_iota(jnp.int32, (BLK, BLK), 1)
    order = parity_sign(jnp.bitwise_and(down, across))
    upper = jnp.bitwise_and(jnp.right_shift(me_ref[0], full - 1), 1)
    own_order = order * (1 - 2 * upper)
    for chunk in range(chunks):
        for copy in fetch(chunk):
            copy.wait()
        if chunk + AHEAD < chunks:
            for copy in fetch(chunk + AHEAD):
                copy.start()
        for block in range(chunk * step // BLK, (chunk + 1) * step // BLK):
            at = block * BLK
            weights, values = [], []
            for signed, sign_ref, buffer_ref in zip((own_order, order), (signs_ref, other_signs_ref), buffer_refs):
                row = sign_ref.shape[0] - rows // BLK + block
                weights += [(signed * sign_ref[row:row + 1, :]).astype(jnp.float32).astype(jnp.bfloat16)] * 2
                whole = buffer_ref[at:at + BLK, :]
                high = whole.astype(jnp.bfloat16)
                values += [high, (whole - high.astype(jnp.float32)).astype(jnp.bfloat16)]
            mixed = jnp.dot(
                jnp.concatenate(weights, axis=1),
                jnp.concatenate(values, axis=0),
                preferred_element_type=jnp.float32,
            )
            for half in range(2):
                table_ref[pl.ds(2 * at + half, BLK, stride=2), :] = mixed[:, half * cols:(half + 1) * cols]


def join_kernel(*refs):
    *list_refs, out_ref = refs
    for at, list_ref in enumerate(list_refs):
        rows = list_ref.shape[0]
        out_ref[at * rows:(at + 1) * rows, :] = list_ref[...]


def specs(smem, vmem):
    return [pl.BlockSpec(memory_space=pltpu.SMEM)] * smem + [pl.BlockSpec(memory_space=pltpu.VMEM)] * vmem


def floats(*shape):
    return jax.ShapeDtypeStruct(shape, jnp.float32)


def transform(full, me, matrix, signs, other_matrix, other_signs):
    rows, width = matrix.shape
    chunks = 8
    return pl.pallas_call(
        functools.partial(transform_kernel, full, chunks),
        in_specs=specs(1, 2) + [pl.BlockSpec(memory_space=pl.ANY)] * 2,
        out_specs=specs(0, 1)[0],
        out_shape=floats(2 * rows, width // 2),
        scratch_shapes=[pltpu.VMEM((rows, width), jnp.float32)] * 2 + [pltpu.SemaphoreType.DMA((chunks, 2))],
        compiler_params=pltpu.CompilerParams(vmem_limit_bytes=WIDE),
        cost_estimate=pl.CostEstimate(
            flops=16 * rows * BLK * width, bytes_accessed=12 * rows * width, transcendentals=0
        ),
        name="transform",
    )(me, signs, other_signs, matrix, other_matrix)


def pick_rows(geometry, me, list_refs, table_ref, out_ref, row, pick, start, slots):
    stride, full, scale = geometry
    unroll = 32
    group = jnp.right_shift(me, full)
    sign = parity_sign(jnp.bitwise_and(jnp.bitwise_xor(group, pick), group)).astype(jnp.float32) * scale
    list_ref = list_refs[pick % 4]
    base = pick // 4 * stride
    live = jnp.clip(list_ref[base + stride - BLK] - start, 0, slots)

    def body(step, carry):
        first = step * unroll
        for u in range(unroll):
            out_ref[row + first + u] = table_ref[list_ref[base + start + first + u]] * sign
        return carry

    lax.fori_loop(0, pl.cdiv(live, unroll), body, 0)


def distances(x, y):
    return [x | y << 1 | a << 2 | b << 3 for a in range(2) for b in range(2)]


def gather(geometry, parts, me_ref, *refs):
    list_refs, table_ref, out_refs = refs[:4], refs[4], refs[-len(parts):]
    for (start, slots, picks), out_ref in zip(parts, out_refs):
        for at, pick in enumerate(picks):
            pick_rows(geometry, me_ref[0], list_refs, table_ref, out_ref, at * slots, pick, start, slots)


def call(kernel, name, scalars, arrays, outs, after=(), scratch=(), flops=0):
    moved = 4 * sum(x.size for x in arrays) + 4 * sum(x.size for x in outs)
    return pl.pallas_call(
        kernel,
        in_specs=specs(len(scalars), len(arrays)) + [pl.BlockSpec(memory_space=pl.ANY)] * len(after),
        out_specs=specs(0, len(outs)),
        out_shape=list(outs),
        scratch_shapes=list(scratch),
        compiler_params=pltpu.CompilerParams(vmem_limit_bytes=GRANT),
        cost_estimate=pl.CostEstimate(flops=flops, bytes_accessed=moved, transcendentals=0),
        name=name,
    )(*scalars, *arrays, *after)


def gram_kernel(ry_ref, live_ref, *refs):
    *part_refs, sketch_ref, on_ref, mine_ref, next_ref, rows_ref, blocks_ref = refs
    slots, cols = rows_ref.shape[0] // 2, rows_ref.shape[1]
    start = 0
    for near_ref, add_ref in zip(part_refs[::2], part_refs[1::2]):
        rows_ref[start:start + near_ref.shape[0], :] = near_ref[...] + add_ref[...]
        start += near_ref.shape[0]
    values = jnp.concatenate([rows_ref[pl.ds(half, slots, stride=2), :] for half in range(2)], axis=1)
    live = lax.broadcasted_iota(jnp.int32, values.shape, 0) < live_ref[0]
    values = jnp.where(live, values, 0.0)
    sketch_ref[...] = values
    high = values.astype(jnp.bfloat16)
    low = (values - high.astype(jnp.float32)).astype(jnp.bfloat16)
    total = lax.dot_general(
        jnp.concatenate([high, high, low], axis=0),
        jnp.concatenate([high, low, high], axis=0),
        (((0,), (0,)), ((), ())),
        preferred_element_type=jnp.float32,
    )
    for block in range(4):
        a, b = block // 2, block % 2
        blocks_ref[block] = total[a * cols:(a + 1) * cols, b * cols:(b + 1) * cols]
    ry = ry_ref[0]
    mine_ref[...] = blocks_ref[ry]
    on_ref[:cols, :] = blocks_ref[jnp.bitwise_xor(ry, 1)]
    next_ref[...] = blocks_ref[jnp.bitwise_xor(ry, 2)]
    on_ref[cols:, :] = blocks_ref[jnp.bitwise_xor(ry, 3)]


def local(matrix, signs, indices, counts):
    rows, width = matrix.shape
    slots = indices.shape[0]
    cols = width // 2
    tail = slots // 4
    head = slots - tail
    first = slots // 8 * 3
    size_x = lax.axis_size("rx")
    size_y = lax.axis_size("ry")
    size = size_x * size_y
    full = size.bit_length() - 1 - REST
    assert full >= 1 and size_y == 4
    ry = lax.axis_index("ry")
    me = lax.axis_index("rx") * size_y + ry
    scale = 1.0 / (size * BLK) ** 0.5
    stride = slots + BLK

    me_one = me.astype(jnp.int32).reshape(1)
    signs = signs.reshape(rows // BLK, BLK)
    if full > 1:
        matrix = (matrix.reshape(rows // BLK, BLK, width) * signs[:, :, None].astype(jnp.float32)).reshape(rows, width)
        signs = jnp.ones_like(signs)
    for bit in range(full - 1):
        other = swap(matrix, 1 << bit)
        matrix = jnp.where(jnp.bitwise_and(jnp.right_shift(me, bit), 1) == 1, other - matrix, matrix + other)
    own = jnp.concatenate([indices, jnp.broadcast_to(counts, (BLK,)), signs.reshape(-1)]).reshape(-1, BLK)
    own = lax.optimization_barrier(own)
    own_list = own[:stride // BLK]
    last = 1 << (full - 1)
    table = transform(full, me_one, matrix, own, swap(matrix, last), swap(own, last)).reshape(rows, 2, cols)
    column_lists = [own_list] + [swap(own_list, step << full) for step in (4, 8, 12)]
    (joined,) = call(
        join_kernel, "join", (), column_lists, (jax.ShapeDtypeStruct((4 * stride // BLK, BLK), jnp.int32),)
    )
    lists = [joined.reshape(-1)] + [swap(joined, step << full).reshape(-1) for step in (1, 2, 3)]

    geometry = (stride, full, scale)
    scalars = (me_one, *lists)

    def gathered(name, parts, after=()):
        outs = [floats(slots * len(picks), 2, cols) for _, slots, picks in parts]
        kernel = functools.partial(gather, geometry, parts)
        return [x.reshape(-1, cols) for x in call(kernel, name, scalars, (table,), outs, after=after)]

    a, b = (0, first), (first, head - first)
    *fars, end_on = gathered(
        "gather_far",
        [
            (*a, distances(1, 0) + distances(1, 1)),
            (*b, distances(0, 1) + distances(1, 1)),
            (head, tail, [z + near for z in (4, 12) for near in (0, 2, 1, 3)]),
        ],
    )
    end_add = swap(end_on, 4 << full)
    ends = gathered("gather_end", [(head, tail, [z + near for near in (0, 2, 1, 3)]) for z in (0, 8)])
    nears = gathered(
        "gather_near",
        [(*a, distances(0, 0)), (*a, distances(0, 1)), (*b, distances(0, 0)), (*b, distances(1, 0))],
        after=(end_add,),
    )

    def halved(value):
        middle = value.shape[0] // 2
        return value[:middle], value[middle:]

    for bits in (8, 1, 2):
        end, end_on = (own + add for own, add in zip(ends, halved(end_add)))
        end_add = swap(end_on, bits << full)
        ends = halved(end)

    finals = []
    for stays, far, steps in ((nears[:2], fars[0], (1, 2, 4, 8)), (nears[2:], fars[1], (2, 1, 4, 8))):
        for step in steps[:-1]:
            near, far = (own + add for own, add in zip(stays, halved(swap(far, step << full))))
            stays = halved(near)
        finals += [near, swap(far, steps[-1] << full)]

    sketch, on, block, far_block = call(
        gram_kernel,
        "gram",
        (ry.astype(jnp.int32).reshape(1), counts),
        (*finals, end, end_add),
        (floats(slots, width), floats(2 * cols, cols), floats(cols, cols), floats(cols, cols)),
        scratch=[pltpu.VMEM((2 * slots, cols), jnp.float32), pltpu.VMEM((4, cols, cols), jnp.float32)],
        flops=6 * slots * width * width,
    )
    got = swap(on, 1)
    block, far_block = block + got[:cols], far_block + got[cols:]
    block = block + swap(far_block, 2) + swap(block, size_y) + swap(far_block, 2 + size_y)
    at, bits = 1, size_x.bit_length() - 1
    while at < bits:
        together = min(2, bits - at)
        block = sum([swap(block, size_y * (step << at)) for step in range(1, 2**together)], block)
        at += together
    return sketch, (block * (1.0 / (size * slots)))[None]


def solution(mesh):
    in_specs = (P(("rx", "ry"), None), P(("rx", "ry")), P(("rx", "ry")), P(("rx", "ry")))
    out_specs = (P(("rx", "ry"), None), P("ry", None, None))
    return jax.shard_map(local, mesh=mesh, in_specs=in_specs, out_specs=out_specs, check_vma=False)
```

```python
import functools

import jax
import jax.numpy as jnp
from jax import lax
from jax.experimental import pallas as pl
from jax.experimental.pallas import tpu as pltpu
from jax.sharding import PartitionSpec as P

BLK = 128
MESH_AXES = ("rx", "ry")
GRANT = 12 * 2**20
WIDE = 46 * 2**20
AHEAD = 3
REST = 4


def swap(value, bits):
    size = lax.axis_size("rx") * lax.axis_size("ry")
    return lax.ppermute(value, MESH_AXES, [(i, i ^ bits) for i in range(size)])


def parity_sign(both):
    for shift in (4, 2, 1):
        both = jnp.bitwise_xor(both, jnp.right_shift(both, shift))
    return 1 - 2 * jnp.bitwise_and(both, 1)


def transform_kernel(full, chunks, me_ref, signs_ref, other_signs_ref, *refs):
    matrix_refs, table_ref, buffer_refs, sems = refs[:2], refs[2], refs[3:5], refs[5]
    rows, cols = table_ref.shape[0] // 2, table_ref.shape[1]
    step = rows // chunks

    def fetch(chunk):
        at = pl.ds(chunk * step, step)
        return [
            pltpu.make_async_copy(matrix_ref.at[at, :], buffer_ref.at[at, :], sems.at[chunk, which])
            for which, (matrix_ref, buffer_ref) in enumerate(zip(matrix_refs, buffer_refs))
        ]

    for chunk in range(AHEAD):
        for copy in fetch(chunk):
            copy.start()
    down = lax.broadcasted_iota(jnp.int32, (BLK, BLK), 0)
    across = lax.broadcasted_iota(jnp.int32, (BLK, BLK), 1)
    order = parity_sign(jnp.bitwise_and(down, across))
    upper = jnp.bitwise_and(jnp.right_shift(me_ref[0], full - 1), 1)
    last = signs_ref.shape[0] - rows // BLK
    signs = signs_ref[last:, :] * (1 - 2 * upper)
    both = (signs * other_signs_ref[last:, :]).astype(jnp.float32).T
    for chunk in range(chunks):
        for copy in fetch(chunk):
            copy.wait()
        if chunk + AHEAD < chunks:
            for copy in fetch(chunk + AHEAD):
                copy.start()
        for block in range(chunk * step // BLK, (chunk + 1) * step // BLK):
            at = block * BLK
            weights = (order * signs[block:block + 1, :]).astype(jnp.float32).astype(jnp.bfloat16)
            own, other = (buffer_ref[at:at + BLK, :] for buffer_ref in buffer_refs)
            values = own + both[:, block:block + 1] * other
            high = values.astype(jnp.bfloat16)
            low = (values - high.astype(jnp.float32)).astype(jnp.bfloat16)
            mixed = jnp.dot(
                jnp.concatenate([weights, weights], axis=1),
                jnp.concatenate([high, low], axis=0),
                preferred_element_type=jnp.float32,
            )
            for half in range(2):
                table_ref[pl.ds(2 * at + half, BLK, stride=2), :] = mixed[:, half * cols:(half + 1) * cols]


def join_kernel(*refs):
    *list_refs, out_ref = refs
    for at, list_ref in enumerate(list_refs):
        rows = list_ref.shape[0]
        out_ref[at * rows:(at + 1) * rows, :] = list_ref[...]


def specs(smem, vmem):
    return [pl.BlockSpec(memory_space=pltpu.SMEM)] * smem + [pl.BlockSpec(memory_space=pltpu.VMEM)] * vmem


def floats(*shape):
    return jax.ShapeDtypeStruct(shape, jnp.float32)


def transform(full, me, matrix, signs, other_matrix, other_signs):
    rows, width = matrix.shape
    chunks = 8
    return pl.pallas_call(
        functools.partial(transform_kernel, full, chunks),
        in_specs=specs(1, 2) + [pl.BlockSpec(memory_space=pl.ANY)] * 2,
        out_specs=specs(0, 1)[0],
        out_shape=floats(2 * rows, width // 2),
        scratch_shapes=[pltpu.VMEM((rows, width), jnp.float32)] * 2 + [pltpu.SemaphoreType.DMA((chunks, 2))],
        compiler_params=pltpu.CompilerParams(vmem_limit_bytes=WIDE),
        cost_estimate=pl.CostEstimate(
            flops=16 * rows * BLK * width, bytes_accessed=12 * rows * width, transcendentals=0
        ),
        name="transform",
    )(me, signs, other_signs, matrix, other_matrix)


def pick_rows(geometry, me, list_refs, table_ref, out_ref, row, pick, start, slots):
    stride, full, scale = geometry
    unroll = max(u for u in range(1, 33) if slots % u == 0)
    group = jnp.right_shift(me, full)
    sign = parity_sign(jnp.bitwise_and(jnp.bitwise_xor(group, pick), group)).astype(jnp.float32) * scale
    list_ref = list_refs[pick % 4]
    base = pick // 4 * stride
    live = jnp.clip(list_ref[base + stride - BLK] - start, 0, slots)

    def body(step, carry):
        first = step * unroll
        for u in range(unroll):
            out_ref[row + first + u] = table_ref[list_ref[base + start + first + u]] * sign
        return carry

    lax.fori_loop(0, pl.cdiv(live, unroll), body, 0)


def distances(x, y):
    return [x | y << 1 | a << 2 | b << 3 for a in range(2) for b in range(2)]


def gather(geometry, parts, me_ref, *refs):
    list_refs, table_ref, out_refs = refs[:4], refs[4], refs[-len(parts):]
    for (start, slots, picks), out_ref in zip(parts, out_refs):
        for at, pick in enumerate(picks):
            pick_rows(geometry, me_ref[0], list_refs, table_ref, out_ref, at * slots, pick, start, slots)


def call(kernel, name, scalars, arrays, outs, after=(), scratch=(), flops=0):
    moved = 4 * sum(x.size for x in arrays) + 4 * sum(x.size for x in outs)
    return pl.pallas_call(
        kernel,
        in_specs=specs(len(scalars), len(arrays)) + [pl.BlockSpec(memory_space=pl.ANY)] * len(after),
        out_specs=specs(0, len(outs)),
        out_shape=list(outs),
        scratch_shapes=list(scratch),
        compiler_params=pltpu.CompilerParams(vmem_limit_bytes=GRANT),
        cost_estimate=pl.CostEstimate(flops=flops, bytes_accessed=moved, transcendentals=0),
        name=name,
    )(*scalars, *arrays, *after)


def gram_kernel(ry_ref, live_ref, *refs):
    *part_refs, sketch_ref, on_ref, mine_ref, next_ref, rows_ref, blocks_ref = refs
    slots, cols = rows_ref.shape[0] // 2, rows_ref.shape[1]
    start = 0
    for near_ref, add_ref in zip(part_refs[::2], part_refs[1::2]):
        rows_ref[start:start + near_ref.shape[0], :] = near_ref[...] + add_ref[...]
        start += near_ref.shape[0]
    values = jnp.concatenate([rows_ref[pl.ds(half, slots, stride=2), :] for half in range(2)], axis=1)
    live = lax.broadcasted_iota(jnp.int32, values.shape, 0) < live_ref[0]
    values = jnp.where(live, values, 0.0)
    sketch_ref[...] = values
    high = values.astype(jnp.bfloat16)
    low = (values - high.astype(jnp.float32)).astype(jnp.bfloat16)
    total = lax.dot_general(
        jnp.concatenate([high, high, low], axis=0),
        jnp.concatenate([high, low, high], axis=0),
        (((0,), (0,)), ((), ())),
        preferred_element_type=jnp.float32,
    )
    for block in range(4):
        a, b = block // 2, block % 2
        blocks_ref[block] = total[a * cols:(a + 1) * cols, b * cols:(b + 1) * cols]
    ry = ry_ref[0]
    mine_ref[...] = blocks_ref[ry]
    on_ref[:cols, :] = blocks_ref[jnp.bitwise_xor(ry, 1)]
    next_ref[...] = blocks_ref[jnp.bitwise_xor(ry, 2)]
    on_ref[cols:, :] = blocks_ref[jnp.bitwise_xor(ry, 3)]


def local(matrix, signs, indices, counts):
    rows, width = matrix.shape
    slots = indices.shape[0]
    cols = width // 2
    tail = slots // 32 * 9
    head = slots - tail
    first = slots // 8 * 3
    size_x = lax.axis_size("rx")
    size_y = lax.axis_size("ry")
    size = size_x * size_y
    full = size.bit_length() - 1 - REST
    assert full >= 1 and size_y == 4
    ry = lax.axis_index("ry")
    me = lax.axis_index("rx") * size_y + ry
    scale = 1.0 / (size * BLK) ** 0.5
    stride = slots + BLK

    me_one = me.astype(jnp.int32).reshape(1)
    signs = signs.reshape(rows // BLK, BLK)
    if full > 1:
        matrix = (matrix.reshape(rows // BLK, BLK, width) * signs[:, :, None].astype(jnp.float32)).reshape(rows, width)
        signs = jnp.ones_like(signs)
    for bit in range(full - 1):
        other = swap(matrix, 1 << bit)
        matrix = jnp.where(jnp.bitwise_and(jnp.right_shift(me, bit), 1) == 1, other - matrix, matrix + other)
    own = jnp.concatenate([indices, jnp.broadcast_to(counts, (BLK,)), signs.reshape(-1)]).reshape(-1, BLK)
    own = lax.optimization_barrier(own)
    own_list = own[:stride // BLK]
    last = 1 << (full - 1)
    table = transform(full, me_one, matrix, own, swap(matrix, last), swap(own, last)).reshape(rows, 2, cols)
    column_lists = [own_list] + [swap(own_list, step << full) for step in (4, 8, 12)]
    (joined,) = call(
        join_kernel, "join", (), column_lists, (jax.ShapeDtypeStruct((4 * stride // BLK, BLK), jnp.int32),)
    )
    lists = [joined.reshape(-1)] + [swap(joined, step << full).reshape(-1) for step in (1, 2, 3)]

    geometry = (stride, full, scale)
    scalars = (me_one, *lists)

    def gathered(name, parts, after=()):
        outs = [floats(slots * len(picks), 2, cols) for _, slots, picks in parts]
        kernel = functools.partial(gather, geometry, parts)
        return [x.reshape(-1, cols) for x in call(kernel, name, scalars, (table,), outs, after=after)]

    a, b = (0, first), (first, head - first)
    *fars, end_on = gathered(
        "gather_far",
        [
            (*a, distances(1, 0) + distances(1, 1)),
            (*b, distances(0, 1) + distances(1, 1)),
            (head, tail, [z + near for z in (4, 12) for near in (0, 2, 1, 3)]),
        ],
    )
    end_add = swap(end_on, 4 << full)
    ends = gathered("gather_end", [(head, tail, [z + near for near in (0, 2, 1, 3)]) for z in (0, 8)])
    nears = gathered(
        "gather_near",
        [(*a, distances(0, 0)), (*a, distances(0, 1)), (*b, distances(0, 0)), (*b, distances(1, 0))],
        after=(end_add,),
    )

    def halved(value):
        middle = value.shape[0] // 2
        return value[:middle], value[middle:]

    for bits in (8, 1, 2):
        end, end_on = (own + add for own, add in zip(ends, halved(end_add)))
        end_add = swap(end_on, bits << full)
        ends = halved(end)

    finals = []
    for stays, far, steps in ((nears[:2], fars[0], (1, 2, 4, 8)), (nears[2:], fars[1], (2, 1, 4, 8))):
        for step in steps[:-1]:
            near, far = (own + add for own, add in zip(stays, halved(swap(far, step << full))))
            stays = halved(near)
        finals += [near, swap(far, steps[-1] << full)]

    sketch, on, block, far_block = call(
        gram_kernel,
        "gram",
        (ry.astype(jnp.int32).reshape(1), counts),
        (*finals, end, end_add),
        (floats(slots, width), floats(2 * cols, cols), floats(cols, cols), floats(cols, cols)),
        scratch=[pltpu.VMEM((2 * slots, cols), jnp.float32), pltpu.VMEM((4, cols, cols), jnp.float32)],
        flops=6 * slots * width * width,
    )
    got = swap(on, 1)
    block, far_block = block + got[:cols], far_block + got[cols:]
    block = block + swap(far_block, 2) + swap(block, size_y) + swap(far_block, 2 + size_y)
    at, bits = 1, size_x.bit_length() - 1
    while at < bits:
        together = min(2, bits - at)
        block = sum([swap(block, size_y * (step << at)) for step in range(1, 2**together)], block)
        at += together
    return sketch, (block * (1.0 / (size * slots)))[None]


def solution(mesh):
    in_specs = (P(("rx", "ry"), None), P(("rx", "ry")), P(("rx", "ry")), P(("rx", "ry")))
    out_specs = (P(("rx", "ry"), None), P("ry", None, None))
    return jax.shard_map(local, mesh=mesh, in_specs=in_specs, out_specs=out_specs, check_vma=False)
```

```python
import functools

import jax
import jax.numpy as jnp
from jax import lax
from jax.experimental import pallas as pl
from jax.experimental.pallas import tpu as pltpu
from jax.sharding import PartitionSpec as P

BLK = 128
MESH_AXES = ("rx", "ry")
GRANT = 12 * 2**20
WIDE = 46 * 2**20
AHEAD = 2
REST = 4


def swap(value, bits):
    size = lax.axis_size("rx") * lax.axis_size("ry")
    return lax.ppermute(value, MESH_AXES, [(i, i ^ bits) for i in range(size)])


def parity_sign(both):
    for shift in (4, 2, 1):
        both = jnp.bitwise_xor(both, jnp.right_shift(both, shift))
    return 1 - 2 * jnp.bitwise_and(both, 1)


def transform_kernel(full, chunks, me_ref, signs_ref, other_signs_ref, *refs):
    matrix_refs, table_ref, buffer_refs, sems = refs[:2], refs[2], refs[3:5], refs[5]
    rows, cols = table_ref.shape[0] // 2, table_ref.shape[1]
    step = rows // chunks

    def fetch(chunk):
        at = pl.ds(chunk * step, step)
        return [
            pltpu.make_async_copy(matrix_ref.at[at, :], buffer_ref.at[at, :], sems.at[chunk, which])
            for which, (matrix_ref, buffer_ref) in enumerate(zip(matrix_refs, buffer_refs))
        ]

    for chunk in range(AHEAD):
        for copy in fetch(chunk):
            copy.start()
    down = lax.broadcasted_iota(jnp.int32, (BLK, BLK), 0)
    across = lax.broadcasted_iota(jnp.int32, (BLK, BLK), 1)
    order = parity_sign(jnp.bitwise_and(down, across))
    upper = jnp.bitwise_and(jnp.right_shift(me_ref[0], full - 1), 1)
    last = signs_ref.shape[0] - rows // BLK
    signs = signs_ref[last:, :] * (1 - 2 * upper)
    both = (signs * other_signs_ref[last:, :]).astype(jnp.float32).T
    for chunk in range(chunks):
        for copy in fetch(chunk):
            copy.wait()
        if chunk + AHEAD < chunks:
            for copy in fetch(chunk + AHEAD):
                copy.start()
        for block in range(chunk * step // BLK, (chunk + 1) * step // BLK):
            at = block * BLK
            weights = (order * signs[block:block + 1, :]).astype(jnp.float32).astype(jnp.bfloat16)
            own, other = (buffer_ref[at:at + BLK, :] for buffer_ref in buffer_refs)
            values = own + both[:, block:block + 1] * other
            high = values.astype(jnp.bfloat16)
            low = (values - high.astype(jnp.float32)).astype(jnp.bfloat16)
            mixed = jnp.dot(
                jnp.concatenate([weights, weights], axis=1),
                jnp.concatenate([high, low], axis=0),
                preferred_element_type=jnp.float32,
            )
            for half in range(2):
                table_ref[pl.ds(2 * at + half, BLK, stride=2), :] = mixed[:, half * cols:(half + 1) * cols]


def join_kernel(*refs):
    *list_refs, out_ref = refs
    for at, list_ref in enumerate(list_refs):
        rows = list_ref.shape[0]
        out_ref[at * rows:(at + 1) * rows, :] = list_ref[...]


def specs(smem, vmem):
    return [pl.BlockSpec(memory_space=pltpu.SMEM)] * smem + [pl.BlockSpec(memory_space=pltpu.VMEM)] * vmem


def floats(*shape):
    return jax.ShapeDtypeStruct(shape, jnp.float32)


def transform(full, me, matrix, signs, other_matrix, other_signs):
    rows, width = matrix.shape
    chunks = 4
    return pl.pallas_call(
        functools.partial(transform_kernel, full, chunks),
        in_specs=specs(1, 2) + [pl.BlockSpec(memory_space=pl.ANY)] * 2,
        out_specs=specs(0, 1)[0],
        out_shape=floats(2 * rows, width // 2),
        scratch_shapes=[pltpu.VMEM((rows, width), jnp.float32)] * 2 + [pltpu.SemaphoreType.DMA((chunks, 2))],
        compiler_params=pltpu.CompilerParams(vmem_limit_bytes=WIDE),
        cost_estimate=pl.CostEstimate(
            flops=16 * rows * BLK * width, bytes_accessed=12 * rows * width, transcendentals=0
        ),
        name="transform",
    )(me, signs, other_signs, matrix, other_matrix)


def pick_rows(geometry, me, list_refs, table_ref, out_ref, row, pick, start, slots):
    stride, full, scale = geometry
    unroll = max(u for u in range(1, 33) if slots % u == 0)
    group = jnp.right_shift(me, full)
    sign = parity_sign(jnp.bitwise_and(jnp.bitwise_xor(group, pick), group)).astype(jnp.float32) * scale
    list_ref = list_refs[pick % 4]
    base = pick // 4 * stride
    live = jnp.clip(list_ref[base + stride - BLK] - start, 0, slots)

    def body(step, carry):
        first = step * unroll
        for u in range(unroll):
            out_ref[row + first + u] = table_ref[list_ref[base + start + first + u]] * sign
        return carry

    lax.fori_loop(0, pl.cdiv(live, unroll), body, 0)


def distances(x, y):
    return [x | y << 1 | a << 2 | b << 3 for a in range(2) for b in range(2)]


def gather(geometry, parts, me_ref, *refs):
    list_refs, table_ref, out_refs = refs[:4], refs[4], refs[-len(parts):]
    for (start, slots, picks), out_ref in zip(parts, out_refs):
        for at, pick in enumerate(picks):
            pick_rows(geometry, me_ref[0], list_refs, table_ref, out_ref, at * slots, pick, start, slots)


def call(kernel, name, scalars, arrays, outs, after=(), scratch=(), flops=0):
    moved = 4 * sum(x.size for x in arrays) + 4 * sum(x.size for x in outs)
    return pl.pallas_call(
        kernel,
        in_specs=specs(len(scalars), len(arrays)) + [pl.BlockSpec(memory_space=pl.ANY)] * len(after),
        out_specs=specs(0, len(outs)),
        out_shape=list(outs),
        scratch_shapes=list(scratch),
        compiler_params=pltpu.CompilerParams(vmem_limit_bytes=GRANT),
        cost_estimate=pl.CostEstimate(flops=flops, bytes_accessed=moved, transcendentals=0),
        name=name,
    )(*scalars, *arrays, *after)


def sum_kernel(first_ref, first_add_ref, second_ref, second_add_ref, *refs):
    near_ref, far_ref = refs[-2:]
    rows = first_ref.shape[0] // 2
    for at, (own_ref, add_ref) in enumerate(((first_ref, first_add_ref), (second_ref, second_add_ref))):
        total = own_ref[...] + add_ref[...]
        near_ref[at * rows:(at + 1) * rows, :] = total[:rows]
        far_ref[at * rows:(at + 1) * rows, :] = total[rows:]


def gram_kernel(ry_ref, list_ref, *refs):
    *part_refs, sketch_ref, on_ref, mine_ref, next_ref, rows_ref, blocks_ref = refs
    slots, cols = rows_ref.shape[0] // 2, rows_ref.shape[1]
    start = 0
    for near_ref, add_ref in zip(part_refs[::2], part_refs[1::2]):
        rows_ref[start:start + near_ref.shape[0], :] = near_ref[...] + add_ref[...]
        start += near_ref.shape[0]
    values = jnp.concatenate([rows_ref[pl.ds(half, slots, stride=2), :] for half in range(2)], axis=1)
    live = lax.broadcasted_iota(jnp.int32, values.shape, 0) < list_ref[slots]
    values = jnp.where(live, values, 0.0)
    sketch_ref[...] = values
    high = values.astype(jnp.bfloat16)
    low = (values - high.astype(jnp.float32)).astype(jnp.bfloat16)
    total = lax.dot_general(
        jnp.concatenate([high, high, low], axis=0),
        jnp.concatenate([high, low, high], axis=0),
        (((0,), (0,)), ((), ())),
        preferred_element_type=jnp.float32,
    )
    for block in range(4):
        a, b = block // 2, block % 2
        blocks_ref[block] = total[a * cols:(a + 1) * cols, b * cols:(b + 1) * cols]
    ry = ry_ref[0]
    mine_ref[...] = blocks_ref[ry]
    on_ref[:cols, :] = blocks_ref[jnp.bitwise_xor(ry, 1)]
    next_ref[...] = blocks_ref[jnp.bitwise_xor(ry, 2)]
    on_ref[cols:, :] = blocks_ref[jnp.bitwise_xor(ry, 3)]


def local(matrix, signs, indices, counts):
    rows, width = matrix.shape
    slots = indices.shape[0]
    cols = width // 2
    tail = slots // 16 * 5
    head = slots - tail
    first = head // 2
    size_x = lax.axis_size("rx")
    size_y = lax.axis_size("ry")
    size = size_x * size_y
    full = size.bit_length() - 1 - REST
    assert full >= 1 and size_y == 4
    ry = lax.axis_index("ry")
    me = lax.axis_index("rx") * size_y + ry
    scale = 1.0 / (size * BLK) ** 0.5
    stride = slots + BLK

    me_one = me.astype(jnp.int32).reshape(1)
    signs = signs.reshape(rows // BLK, BLK)
    if full > 1:
        matrix = (matrix.reshape(rows // BLK, BLK, width) * signs[:, :, None].astype(jnp.float32)).reshape(rows, width)
        signs = jnp.ones_like(signs)
    for bit in range(full - 1):
        other = swap(matrix, 1 << bit)
        matrix = jnp.where(jnp.bitwise_and(jnp.right_shift(me, bit), 1) == 1, other - matrix, matrix + other)
    own = jnp.concatenate([indices, jnp.pad(counts, (0, BLK - 1)), signs.reshape(-1)]).reshape(-1, BLK)
    own = lax.optimization_barrier(own)
    own_list = own[:stride // BLK]
    last = 1 << (full - 1)
    table = transform(full, me_one, matrix, own, swap(matrix, last), swap(own, last)).reshape(rows, 2, cols)
    column_lists = [own_list] + [swap(own_list, step << full) for step in (4, 8, 12)]
    (joined,) = call(
        join_kernel, "join", (), column_lists, (jax.ShapeDtypeStruct((4 * stride // BLK, BLK), jnp.int32),)
    )
    lists = [joined.reshape(-1)] + [swap(joined, step << full).reshape(-1) for step in (1, 2, 3)]

    geometry = (stride, full, scale)
    scalars = (me_one, *lists)

    def gathered(name, parts, after=()):
        outs = [floats(slots * len(picks), 2, cols) for _, slots, picks in parts]
        kernel = functools.partial(gather, geometry, parts)
        return [x.reshape(-1, cols) for x in call(kernel, name, scalars, (table,), outs, after=after)]

    a, b = (0, first), (first, head - first)
    xy = (0, 2, 1, 3)
    routes = (((4, 12), (0, 8)), ((8, 12), (0, 4)))
    ends = [(head + at * tail // 2, tail // 2) for at in range(2)]
    *fars, end_on, other_end_on = gathered(
        "gather_far",
        [
            (*a, distances(1, 0) + distances(1, 1)),
            (*b, distances(0, 1) + distances(1, 1)),
            *((*end, [z + near for z in sent for near in xy]) for end, (sent, _) in zip(ends, routes)),
        ],
    )
    end_adds = [swap(end_on, 4 << full), swap(other_end_on, 8 << full)]
    end_stays = gathered(
        "gather_end",
        [(*end, [z + near for near in xy]) for end, (_, stays) in zip(ends, routes) for z in stays],
        after=(end_adds[0],),
    )
    nears = gathered(
        "gather_near",
        [(*a, distances(0, 0)), (*a, distances(0, 1)), (*b, distances(0, 0)), (*b, distances(1, 0))],
        after=(end_adds[0],),
    )

    def halved(value):
        middle = value.shape[0] // 2
        return value[:middle], value[middle:]

    finals, seconds = [], []
    for stays, far, steps in ((nears[:2], fars[0], (1, 2, 4, 8)), (nears[2:], fars[1], (2, 1, 4, 8))):
        for at, step in enumerate(steps[:-1]):
            near, far = (own + add for own, add in zip(stays, halved(swap(far, step << full))))
            stays = halved(near)
            if at == 2 and not seconds:
                seconds.append(far)
        finals += [near, swap(far, steps[-1] << full)]

    pairs = []
    for stays, add, step in zip((end_stays[:2], end_stays[2:]), end_adds, (8, 4)):
        near, far = (own + got for own, got in zip(stays, halved(add)))
        pairs += [near, swap(far, step << full)]
    middle = floats(4 * tail, cols)
    end, end_on = call(sum_kernel, "sum_ends", (), pairs, (middle, middle), after=seconds)
    own, got = ([part[at * tail:(at + 1) * tail] for at in range(4)] for part in (end, swap(end_on, 1 << full)))
    last_parts = [
        jnp.concatenate([own[0] + got[0], own[2] + got[2]]),
        swap(jnp.concatenate([own[1] + got[1], own[3] + got[3]]), 2 << full),
    ]

    sketch, on, block, far_block = call(
        gram_kernel,
        "gram",
        (ry.astype(jnp.int32).reshape(1), lists[0]),
        (*finals, *last_parts),
        (floats(slots, width), floats(2 * cols, cols), floats(cols, cols), floats(cols, cols)),
        scratch=[pltpu.VMEM((2 * slots, cols), jnp.float32), pltpu.VMEM((4, cols, cols), jnp.float32)],
        flops=6 * slots * width * width,
    )
    got = swap(on, 1)
    block, far_block = block + got[:cols], far_block + got[cols:]
    block = block + swap(far_block, 2) + swap(block, size_y) + swap(far_block, 2 + size_y)
    at, bits = 1, size_x.bit_length() - 1
    while at < bits:
        together = min(2, bits - at)
        block = sum([swap(block, size_y * (step << at)) for step in range(1, 2**together)], block)
        at += together
    return sketch, (block * (1.0 / (size * slots)))[None]


def solution(mesh):
    in_specs = (P(("rx", "ry"), None), P(("rx", "ry")), P(("rx", "ry")), P(("rx", "ry")))
    out_specs = (P(("rx", "ry"), None), P("ry", None, None))
    return jax.shard_map(local, mesh=mesh, in_specs=in_specs, out_specs=out_specs, check_vma=False)
```

```python
import functools

import jax
import jax.numpy as jnp
from jax import lax
from jax.experimental import pallas as pl
from jax.experimental.pallas import tpu as pltpu
from jax.sharding import PartitionSpec as P

BLK = 128
MESH_AXES = ("rx", "ry")
GRANT = 12 * 2**20
WIDE = 46 * 2**20
AHEAD = 2
REST = 4


def swap(value, bits):
    size = lax.axis_size("rx") * lax.axis_size("ry")
    return lax.ppermute(value, MESH_AXES, [(i, i ^ bits) for i in range(size)])


def parity_sign(both):
    for shift in (4, 2, 1):
        both = jnp.bitwise_xor(both, jnp.right_shift(both, shift))
    return 1 - 2 * jnp.bitwise_and(both, 1)


def transform_kernel(full, chunks, me_ref, signs_ref, other_signs_ref, *refs):
    matrix_refs, table_ref, buffer_refs, sems = refs[:2], refs[2], refs[3:5], refs[5]
    rows, cols = table_ref.shape[0] // 2, table_ref.shape[1]
    step = rows // chunks

    def fetch(chunk):
        at = pl.ds(chunk * step, step)
        return [
            pltpu.make_async_copy(matrix_ref.at[at, :], buffer_ref.at[at, :], sems.at[chunk, which])
            for which, (matrix_ref, buffer_ref) in enumerate(zip(matrix_refs, buffer_refs))
        ]

    for chunk in range(AHEAD):
        for copy in fetch(chunk):
            copy.start()
    down = lax.broadcasted_iota(jnp.int32, (BLK, BLK), 0)
    across = lax.broadcasted_iota(jnp.int32, (BLK, BLK), 1)
    order = parity_sign(jnp.bitwise_and(down, across))
    upper = jnp.bitwise_and(jnp.right_shift(me_ref[0], full - 1), 1)
    last = signs_ref.shape[0] - rows // BLK
    signs = signs_ref[last:, :] * (1 - 2 * upper)
    both = (signs * other_signs_ref[last:, :]).astype(jnp.float32).T
    for chunk in range(chunks):
        for copy in fetch(chunk):
            copy.wait()
        if chunk + AHEAD < chunks:
            for copy in fetch(chunk + AHEAD):
                copy.start()
        for block in range(chunk * step // BLK, (chunk + 1) * step // BLK):
            at = block * BLK
            weights = (order * signs[block:block + 1, :]).astype(jnp.float32).astype(jnp.bfloat16)
            own, other = (buffer_ref[at:at + BLK, :] for buffer_ref in buffer_refs)
            values = own + both[:, block:block + 1] * other
            high = values.astype(jnp.bfloat16)
            low = (values - high.astype(jnp.float32)).astype(jnp.bfloat16)
            mixed = jnp.dot(
                jnp.concatenate([weights, weights], axis=1),
                jnp.concatenate([high, low], axis=0),
                preferred_element_type=jnp.float32,
            )
            for half in range(2):
                table_ref[pl.ds(2 * at + half, BLK, stride=2), :] = mixed[:, half * cols:(half + 1) * cols]


def join_kernel(*refs):
    *list_refs, out_ref = refs
    for at, list_ref in enumerate(list_refs):
        rows = list_ref.shape[0]
        out_ref[at * rows:(at + 1) * rows, :] = list_ref[...]


def specs(smem, vmem):
    return [pl.BlockSpec(memory_space=pltpu.SMEM)] * smem + [pl.BlockSpec(memory_space=pltpu.VMEM)] * vmem


def floats(*shape):
    return jax.ShapeDtypeStruct(shape, jnp.float32)


def transform(full, me, matrix, signs, other_matrix, other_signs):
    rows, width = matrix.shape
    chunks = 4
    return pl.pallas_call(
        functools.partial(transform_kernel, full, chunks),
        in_specs=specs(1, 2) + [pl.BlockSpec(memory_space=pl.ANY)] * 2,
        out_specs=specs(0, 1)[0],
        out_shape=floats(2 * rows, width // 2),
        scratch_shapes=[pltpu.VMEM((rows, width), jnp.float32)] * 2 + [pltpu.SemaphoreType.DMA((chunks, 2))],
        compiler_params=pltpu.CompilerParams(vmem_limit_bytes=WIDE),
        cost_estimate=pl.CostEstimate(
            flops=16 * rows * BLK * width, bytes_accessed=12 * rows * width, transcendentals=0
        ),
        name="transform",
    )(me, signs, other_signs, matrix, other_matrix)


def pick_rows(geometry, me, list_refs, table_ref, out_ref, row, pick, start, slots):
    stride, full, scale = geometry
    unroll = max(u for u in range(1, 33) if slots % u == 0)
    group = jnp.right_shift(me, full)
    sign = parity_sign(jnp.bitwise_and(jnp.bitwise_xor(group, pick), group)).astype(jnp.float32) * scale
    list_ref = list_refs[pick % 4]
    base = pick // 4 * stride
    live = jnp.clip(list_ref[base + stride - BLK] - start, 0, slots)

    def body(step, carry):
        first = step * unroll
        for u in range(unroll):
            out_ref[row + first + u] = table_ref[list_ref[base + start + first + u]] * sign
        return carry

    lax.fori_loop(0, pl.cdiv(live, unroll), body, 0)


def distances(x, y):
    return [x | y << 1 | a << 2 | b << 3 for a in range(2) for b in range(2)]


def gather(geometry, parts, me_ref, *refs):
    list_refs, table_ref, out_refs = refs[:4], refs[4], refs[-len(parts):]
    for (start, slots, picks), out_ref in zip(parts, out_refs):
        for at, pick in enumerate(picks):
            pick_rows(geometry, me_ref[0], list_refs, table_ref, out_ref, at * slots, pick, start, slots)


def call(kernel, name, scalars, arrays, outs, after=(), scratch=(), flops=0):
    moved = 4 * sum(x.size for x in arrays) + 4 * sum(x.size for x in outs)
    return pl.pallas_call(
        kernel,
        in_specs=specs(len(scalars), len(arrays)) + [pl.BlockSpec(memory_space=pl.ANY)] * len(after),
        out_specs=specs(0, len(outs)),
        out_shape=list(outs),
        scratch_shapes=list(scratch),
        compiler_params=pltpu.CompilerParams(vmem_limit_bytes=GRANT),
        cost_estimate=pl.CostEstimate(flops=flops, bytes_accessed=moved, transcendentals=0),
        name=name,
    )(*scalars, *arrays, *after)


def sum_kernel(first_ref, first_add_ref, second_ref, second_add_ref, *refs):
    near_ref, far_ref = refs[-2:]
    rows = first_ref.shape[0] // 2
    for at, (own_ref, add_ref) in enumerate(((first_ref, first_add_ref), (second_ref, second_add_ref))):
        total = own_ref[...] + add_ref[...]
        near_ref[at * rows:(at + 1) * rows, :] = total[:rows]
        far_ref[at * rows:(at + 1) * rows, :] = total[rows:]


def gram_kernel(ry_ref, list_ref, *refs):
    *part_refs, sketch_ref, on_ref, mine_ref, next_ref, rows_ref, blocks_ref = refs
    slots, cols = rows_ref.shape[0] // 2, rows_ref.shape[1]
    start = 0
    for near_ref, add_ref in zip(part_refs[::2], part_refs[1::2]):
        rows_ref[start:start + near_ref.shape[0], :] = near_ref[...] + add_ref[...]
        start += near_ref.shape[0]
    values = jnp.concatenate([rows_ref[pl.ds(half, slots, stride=2), :] for half in range(2)], axis=1)
    live = lax.broadcasted_iota(jnp.int32, values.shape, 0) < list_ref[slots]
    values = jnp.where(live, values, 0.0)
    sketch_ref[...] = values
    high = values.astype(jnp.bfloat16)
    low = (values - high.astype(jnp.float32)).astype(jnp.bfloat16)
    total = lax.dot_general(
        jnp.concatenate([high, high, low], axis=0),
        jnp.concatenate([high, low, high], axis=0),
        (((0,), (0,)), ((), ())),
        preferred_element_type=jnp.float32,
    )
    for block in range(4):
        a, b = block // 2, block % 2
        blocks_ref[block] = total[a * cols:(a + 1) * cols, b * cols:(b + 1) * cols]
    ry = ry_ref[0]
    mine_ref[...] = blocks_ref[ry]
    on_ref[:cols, :] = blocks_ref[jnp.bitwise_xor(ry, 1)]
    next_ref[...] = blocks_ref[jnp.bitwise_xor(ry, 2)]
    on_ref[cols:, :] = blocks_ref[jnp.bitwise_xor(ry, 3)]


def local(matrix, signs, indices, counts):
    rows, width = matrix.shape
    slots = indices.shape[0]
    cols = width // 2
    tail = slots // 16 * 5
    head = slots - tail
    first = head // 2
    size_x = lax.axis_size("rx")
    size_y = lax.axis_size("ry")
    size = size_x * size_y
    full = size.bit_length() - 1 - REST
    assert full >= 1 and size_y == 4
    ry = lax.axis_index("ry")
    me = lax.axis_index("rx") * size_y + ry
    scale = 1.0 / (size * BLK) ** 0.5
    stride = slots + BLK

    me_one = me.astype(jnp.int32).reshape(1)
    signs = signs.reshape(rows // BLK, BLK)
    if full > 1:
        matrix = (matrix.reshape(rows // BLK, BLK, width) * signs[:, :, None].astype(jnp.float32)).reshape(rows, width)
        signs = jnp.ones_like(signs)
    for bit in range(full - 1):
        other = swap(matrix, 1 << bit)
        matrix = jnp.where(jnp.bitwise_and(jnp.right_shift(me, bit), 1) == 1, other - matrix, matrix + other)
    own = jnp.concatenate([indices, jnp.pad(counts, (0, BLK - 1)), signs.reshape(-1)]).reshape(-1, BLK)
    own = lax.optimization_barrier(own)
    own_list = own[:stride // BLK]
    last = 1 << (full - 1)
    table = transform(full, me_one, matrix, own, swap(matrix, last), swap(own, last)).reshape(rows, 2, cols)
    column_lists = [own_list] + [swap(own_list, step << full) for step in (4, 8, 12)]
    (joined,) = call(
        join_kernel, "join", (), column_lists, (jax.ShapeDtypeStruct((4 * stride // BLK, BLK), jnp.int32),)
    )
    lists = [joined.reshape(-1)] + [swap(joined, step << full).reshape(-1) for step in (1, 2, 3)]

    geometry = (stride, full, scale)
    scalars = (me_one, *lists)

    def gathered(name, parts, after=()):
        outs = [floats(slots * len(picks), 2, cols) for _, slots, picks in parts]
        kernel = functools.partial(gather, geometry, parts)
        return [x.reshape(-1, cols) for x in call(kernel, name, scalars, (table,), outs, after=after)]

    a, b = (0, first), (first, head - first)
    xy = (0, 2, 1, 3)
    routes = (((4, 12), (0, 8)), ((8, 12), (0, 4)))
    ends = [(head + at * tail // 2, tail // 2) for at in range(2)]
    *fars, end_on, other_end_on = gathered(
        "gather_far",
        [
            (*a, distances(1, 0) + distances(1, 1)),
            (*b, distances(0, 1) + distances(1, 1)),
            *((*end, [z + near for z in sent for near in xy]) for end, (sent, _) in zip(ends, routes)),
        ],
    )
    end_adds = [swap(end_on, 4 << full), swap(other_end_on, 8 << full)]
    end_stays = gathered(
        "gather_end",
        [(*end, [z + near for near in xy]) for end, (_, stays) in zip(ends, routes) for z in stays],
        after=(end_on,),
    )
    nears = gathered(
        "gather_near",
        [(*a, distances(0, 0)), (*a, distances(0, 1)), (*b, distances(0, 0)), (*b, distances(1, 0))],
        after=(end_on,),
    )

    def halved(value):
        middle = value.shape[0] // 2
        return value[:middle], value[middle:]

    finals, seconds = [], []
    for stays, far, steps in ((nears[:2], fars[0], (1, 2, 4, 8)), (nears[2:], fars[1], (2, 1, 4, 8))):
        for at, step in enumerate(steps[:-1]):
            near, far = (own + add for own, add in zip(stays, halved(swap(far, step << full))))
            stays = halved(near)
            if at == 2 and not seconds:
                seconds.append(far)
        finals += [near, swap(far, steps[-1] << full)]

    pairs = []
    for stays, add, step in zip((end_stays[:2], end_stays[2:]), end_adds, (8, 4)):
        near, far = (own + got for own, got in zip(stays, halved(add)))
        pairs += [near, swap(far, step << full)]
    middle = floats(4 * tail, cols)
    end, end_on = call(sum_kernel, "sum_ends", (), pairs, (middle, middle), after=seconds)
    own, got = ([part[at * tail:(at + 1) * tail] for at in range(4)] for part in (end, swap(end_on, 1 << full)))
    last_parts = [
        jnp.concatenate([own[0] + got[0], own[2] + got[2]]),
        swap(jnp.concatenate([own[1] + got[1], own[3] + got[3]]), 2 << full),
    ]

    sketch, on, block, far_block = call(
        gram_kernel,
        "gram",
        (ry.astype(jnp.int32).reshape(1), lists[0]),
        (*finals, *last_parts),
        (floats(slots, width), floats(2 * cols, cols), floats(cols, cols), floats(cols, cols)),
        scratch=[pltpu.VMEM((2 * slots, cols), jnp.float32), pltpu.VMEM((4, cols, cols), jnp.float32)],
        flops=6 * slots * width * width,
    )
    got = swap(on, 1)
    block, far_block = block + got[:cols], far_block + got[cols:]
    block = block + swap(far_block, 2) + swap(block, size_y) + swap(far_block, 2 + size_y)
    at, bits = 1, size_x.bit_length() - 1
    while at < bits:
        together = min(2, bits - at)
        block = sum([swap(block, size_y * (step << at)) for step in range(1, 2**together)], block)
        at += together
    return sketch, (block * (1.0 / (size * slots)))[None]


def solution(mesh):
    in_specs = (P(("rx", "ry"), None), P(("rx", "ry")), P(("rx", "ry")), P(("rx", "ry")))
    out_specs = (P(("rx", "ry"), None), P("ry", None, None))
    return jax.shard_map(local, mesh=mesh, in_specs=in_specs, out_specs=out_specs, check_vma=False)
```

```python
import functools

import jax
import jax.numpy as jnp
from jax import lax
from jax.experimental import pallas as pl
from jax.experimental.pallas import tpu as pltpu
from jax.sharding import PartitionSpec as P

BLK = 128
MESH_AXES = ("rx", "ry")
GRANT = 12 * 2**20
WIDE = 46 * 2**20
AHEAD = 2
REST = 4


def swap(value, bits):
    size = lax.axis_size("rx") * lax.axis_size("ry")
    return lax.ppermute(value, MESH_AXES, [(i, i ^ bits) for i in range(size)])


def parity_sign(both):
    for shift in (4, 2, 1):
        both = jnp.bitwise_xor(both, jnp.right_shift(both, shift))
    return 1 - 2 * jnp.bitwise_and(both, 1)


def transform_kernel(full, chunks, me_ref, signs_ref, other_signs_ref, *refs):
    matrix_refs, table_ref, buffer_refs, sems = refs[:2], refs[2], refs[3:5], refs[5]
    rows, cols = table_ref.shape[0] // 2, table_ref.shape[1]
    step = rows // chunks

    def fetch(chunk):
        at = pl.ds(chunk * step, step)
        return [
            pltpu.make_async_copy(matrix_ref.at[at, :], buffer_ref.at[at, :], sems.at[chunk, which])
            for which, (matrix_ref, buffer_ref) in enumerate(zip(matrix_refs, buffer_refs))
        ]

    for chunk in range(AHEAD):
        for copy in fetch(chunk):
            copy.start()
    down = lax.broadcasted_iota(jnp.int32, (BLK, BLK), 0)
    across = lax.broadcasted_iota(jnp.int32, (BLK, BLK), 1)
    order = parity_sign(jnp.bitwise_and(down, across))
    upper = jnp.bitwise_and(jnp.right_shift(me_ref[0], full - 1), 1)
    last = signs_ref.shape[0] - rows // BLK
    signs = signs_ref[last:, :] * (1 - 2 * upper)
    both = (signs * other_signs_ref[last:, :]).astype(jnp.float32).T
    for chunk in range(chunks):
        for copy in fetch(chunk):
            copy.wait()
        if chunk + AHEAD < chunks:
            for copy in fetch(chunk + AHEAD):
                copy.start()
        for block in range(chunk * step // BLK, (chunk + 1) * step // BLK):
            at = block * BLK
            weights = (order * signs[block:block + 1, :]).astype(jnp.float32).astype(jnp.bfloat16)
            own, other = (buffer_ref[at:at + BLK, :] for buffer_ref in buffer_refs)
            values = own + both[:, block:block + 1] * other
            high = values.astype(jnp.bfloat16)
            low = (values - high.astype(jnp.float32)).astype(jnp.bfloat16)
            mixed = jnp.dot(
                jnp.concatenate([weights, weights], axis=1),
                jnp.concatenate([high, low], axis=0),
                preferred_element_type=jnp.float32,
            )
            for half in range(2):
                table_ref[pl.ds(2 * at + half, BLK, stride=2), :] = mixed[:, half * cols:(half + 1) * cols]


def join_kernel(*refs):
    *list_refs, out_ref = refs
    for at, list_ref in enumerate(list_refs):
        rows = list_ref.shape[0]
        out_ref[at * rows:(at + 1) * rows, :] = list_ref[...]


def specs(smem, vmem):
    return [pl.BlockSpec(memory_space=pltpu.SMEM)] * smem + [pl.BlockSpec(memory_space=pltpu.VMEM)] * vmem


def floats(*shape):
    return jax.ShapeDtypeStruct(shape, jnp.float32)


def transform(full, me, matrix, signs, other_matrix, other_signs):
    rows, width = matrix.shape
    chunks = 4
    return pl.pallas_call(
        functools.partial(transform_kernel, full, chunks),
        in_specs=specs(1, 2) + [pl.BlockSpec(memory_space=pl.ANY)] * 2,
        out_specs=specs(0, 1)[0],
        out_shape=floats(2 * rows, width // 2),
        scratch_shapes=[pltpu.VMEM((rows, width), jnp.float32)] * 2 + [pltpu.SemaphoreType.DMA((chunks, 2))],
        compiler_params=pltpu.CompilerParams(vmem_limit_bytes=WIDE),
        cost_estimate=pl.CostEstimate(
            flops=16 * rows * BLK * width, bytes_accessed=12 * rows * width, transcendentals=0
        ),
        name="transform",
    )(me, signs, other_signs, matrix, other_matrix)


def pick_rows(geometry, me, list_refs, table_ref, out_ref, row, pick, start, slots):
    stride, full, scale = geometry
    unroll = max(u for u in range(1, 33) if slots % u == 0)
    group = jnp.right_shift(me, full)
    sign = parity_sign(jnp.bitwise_and(jnp.bitwise_xor(group, pick), group)).astype(jnp.float32) * scale
    list_ref = list_refs[pick % 4]
    base = pick // 4 * stride
    live = jnp.clip(list_ref[base + stride - BLK] - start, 0, slots)

    def body(step, carry):
        first = step * unroll
        for u in range(unroll):
            out_ref[row + first + u] = table_ref[list_ref[base + start + first + u]] * sign
        return carry

    lax.fori_loop(0, pl.cdiv(live, unroll), body, 0)


def distances(x, y):
    return [x | y << 1 | a << 2 | b << 3 for a in range(2) for b in range(2)]


def gather(geometry, parts, me_ref, *refs):
    list_refs, table_ref, out_refs = refs[:4], refs[4], refs[-len(parts):]
    for (start, slots, picks), out_ref in zip(parts, out_refs):
        for at, pick in enumerate(picks):
            pick_rows(geometry, me_ref[0], list_refs, table_ref, out_ref, at * slots, pick, start, slots)


def call(kernel, name, scalars, arrays, outs, after=(), scratch=(), flops=0):
    moved = 4 * sum(x.size for x in arrays) + 4 * sum(x.size for x in outs)
    return pl.pallas_call(
        kernel,
        in_specs=specs(len(scalars), len(arrays)) + [pl.BlockSpec(memory_space=pl.ANY)] * len(after),
        out_specs=specs(0, len(outs)),
        out_shape=list(outs),
        scratch_shapes=list(scratch),
        compiler_params=pltpu.CompilerParams(vmem_limit_bytes=GRANT),
        cost_estimate=pl.CostEstimate(flops=flops, bytes_accessed=moved, transcendentals=0),
        name=name,
    )(*scalars, *arrays, *after)


def gram_kernel(ry_ref, list_ref, *refs):
    *part_refs, sketch_ref, on_ref, mine_ref, next_ref, rows_ref, blocks_ref = refs
    slots, cols = rows_ref.shape[0] // 2, rows_ref.shape[1]
    start = 0
    for near_ref, add_ref in zip(part_refs[::2], part_refs[1::2]):
        rows_ref[start:start + near_ref.shape[0], :] = near_ref[...] + add_ref[...]
        start += near_ref.shape[0]
    values = jnp.concatenate([rows_ref[pl.ds(half, slots, stride=2), :] for half in range(2)], axis=1)
    live = lax.broadcasted_iota(jnp.int32, values.shape, 0) < list_ref[slots]
    values = jnp.where(live, values, 0.0)
    sketch_ref[...] = values
    high = values.astype(jnp.bfloat16)
    low = (values - high.astype(jnp.float32)).astype(jnp.bfloat16)
    total = lax.dot_general(
        jnp.concatenate([high, high, low], axis=0),
        jnp.concatenate([high, low, high], axis=0),
        (((0,), (0,)), ((), ())),
        preferred_element_type=jnp.float32,
    )
    for block in range(4):
        a, b = block // 2, block % 2
        blocks_ref[block] = total[a * cols:(a + 1) * cols, b * cols:(b + 1) * cols]
    ry = ry_ref[0]
    mine_ref[...] = blocks_ref[ry]
    on_ref[:cols, :] = blocks_ref[jnp.bitwise_xor(ry, 1)]
    next_ref[...] = blocks_ref[jnp.bitwise_xor(ry, 2)]
    on_ref[cols:, :] = blocks_ref[jnp.bitwise_xor(ry, 3)]


def local(matrix, signs, indices, counts):
    rows, width = matrix.shape
    slots = indices.shape[0]
    cols = width // 2
    tail = slots // 4
    head = slots - tail
    first = slots // 8 * 3
    size_x = lax.axis_size("rx")
    size_y = lax.axis_size("ry")
    size = size_x * size_y
    full = size.bit_length() - 1 - REST
    assert full >= 1 and size_y == 4
    ry = lax.axis_index("ry")
    me = lax.axis_index("rx") * size_y + ry
    scale = 1.0 / (size * BLK) ** 0.5
    stride = slots + BLK

    me_one = me.astype(jnp.int32).reshape(1)
    signs = signs.reshape(rows // BLK, BLK)
    if full > 1:
        matrix = (matrix.reshape(rows // BLK, BLK, width) * signs[:, :, None].astype(jnp.float32)).reshape(rows, width)
        signs = jnp.ones_like(signs)
    for bit in range(full - 1):
        other = swap(matrix, 1 << bit)
        matrix = jnp.where(jnp.bitwise_and(jnp.right_shift(me, bit), 1) == 1, other - matrix, matrix + other)
    own = jnp.concatenate([indices, jnp.pad(counts, (0, BLK - 1)), signs.reshape(-1)]).reshape(-1, BLK)
    own = lax.optimization_barrier(own)
    own_list = own[:stride // BLK]
    last = 1 << (full - 1)
    table = transform(full, me_one, matrix, own, swap(matrix, last), swap(own, last)).reshape(rows, 2, cols)
    column_lists = [own_list] + [swap(own_list, step << full) for step in (4, 8, 12)]
    (joined,) = call(
        join_kernel, "join", (), column_lists, (jax.ShapeDtypeStruct((4 * stride // BLK, BLK), jnp.int32),)
    )
    lists = [joined.reshape(-1)] + [swap(joined, step << full).reshape(-1) for step in (1, 2, 3)]

    geometry = (stride, full, scale)
    scalars = (me_one, *lists)

    def gathered(name, parts, after=()):
        outs = [floats(slots * len(picks), 2, cols) for _, slots, picks in parts]
        kernel = functools.partial(gather, geometry, parts)
        return [x.reshape(-1, cols) for x in call(kernel, name, scalars, (table,), outs, after=after)]

    a, b = (0, first), (first, head - first)
    *fars, end_on = gathered(
        "gather_far",
        [
            (*a, distances(1, 0) + distances(1, 1)),
            (*b, distances(0, 1) + distances(1, 1)),
            (head, tail, [z + near for z in (4, 12) for near in (0, 2, 1, 3)]),
        ],
    )
    end_add = swap(end_on, 4 << full)
    ends = gathered("gather_end", [(head, tail, [z + near for near in (0, 2, 1, 3)]) for z in (0, 8)])
    nears = gathered(
        "gather_near",
        [
            (*a, distances(0, 0)),
            (*a, distances(0, 1)),
            (*b, distances(0, 0)),
            (*b, distances(1, 0)),
        ],
        after=(end_on,),
    )

    def halved(value):
        middle = value.shape[0] // 2
        return value[:middle], value[middle:]

    for bits in (8, 1, 2):
        end, end_on = (own + add for own, add in zip(ends, halved(end_add)))
        end_add = swap(end_on, bits << full)
        ends = halved(end)

    finals = []
    for stays, far, steps in ((nears[:2], fars[0], (1, 2, 4, 8)), (nears[2:], fars[1], (2, 1, 4, 8))):
        for step in steps[:-1]:
            near, far = (own + add for own, add in zip(stays, halved(swap(far, step << full))))
            stays = halved(near)
        finals += [near, swap(far, steps[-1] << full)]

    sketch, on, block, far_block = call(
        gram_kernel,
        "gram",
        (ry.astype(jnp.int32).reshape(1), lists[0]),
        (*finals, end, end_add),
        (floats(slots, width), floats(2 * cols, cols), floats(cols, cols), floats(cols, cols)),
        scratch=[pltpu.VMEM((2 * slots, cols), jnp.float32), pltpu.VMEM((4, cols, cols), jnp.float32)],
        flops=6 * slots * width * width,
    )
    got = swap(on, 1)
    block, far_block = block + got[:cols], far_block + got[cols:]
    block = block + swap(far_block, 2) + swap(block, size_y) + swap(far_block, 2 + size_y)
    at, bits = 1, size_x.bit_length() - 1
    while at < bits:
        together = min(2, bits - at)
        block = sum([swap(block, size_y * (step << at)) for step in range(1, 2**together)], block)
        at += together
    return sketch, (block * (1.0 / (size * slots)))[None]


def solution(mesh):
    in_specs = (P(("rx", "ry"), None), P(("rx", "ry")), P(("rx", "ry")), P(("rx", "ry")))
    out_specs = (P(("rx", "ry"), None), P("ry", None, None))
    return jax.shard_map(local, mesh=mesh, in_specs=in_specs, out_specs=out_specs, check_vma=False)
```

```python
import functools

import jax
import jax.numpy as jnp
from jax import lax
from jax.experimental import pallas as pl
from jax.experimental.pallas import tpu as pltpu
from jax.sharding import PartitionSpec as P

BLK = 128
MESH_AXES = ("rx", "ry")
GRANT = 12 * 2**20
WIDE = 46 * 2**20
AHEAD = 2
REST = 4


def swap(value, bits):
    size = lax.axis_size("rx") * lax.axis_size("ry")
    return lax.ppermute(value, MESH_AXES, [(i, i ^ bits) for i in range(size)])


def parity_sign(both):
    for shift in (4, 2, 1):
        both = jnp.bitwise_xor(both, jnp.right_shift(both, shift))
    return 1 - 2 * jnp.bitwise_and(both, 1)


def transform_kernel(full, chunks, me_ref, signs_ref, other_signs_ref, *refs):
    matrix_refs, table_ref, buffer_refs, sems = refs[:2], refs[2], refs[3:5], refs[5]
    rows, cols = table_ref.shape[0] // 2, table_ref.shape[1]
    step = rows // chunks

    def fetch(chunk):
        at = pl.ds(chunk * step, step)
        return [
            pltpu.make_async_copy(matrix_ref.at[at, :], buffer_ref.at[at, :], sems.at[chunk, which])
            for which, (matrix_ref, buffer_ref) in enumerate(zip(matrix_refs, buffer_refs))
        ]

    for chunk in range(AHEAD):
        for copy in fetch(chunk):
            copy.start()
    down = lax.broadcasted_iota(jnp.int32, (BLK, BLK), 0)
    across = lax.broadcasted_iota(jnp.int32, (BLK, BLK), 1)
    order = parity_sign(jnp.bitwise_and(down, across))
    upper = jnp.bitwise_and(jnp.right_shift(me_ref[0], full - 1), 1)
    last = signs_ref.shape[0] - rows // BLK
    signs = signs_ref[last:, :] * (1 - 2 * upper)
    both = (signs * other_signs_ref[last:, :]).astype(jnp.float32).T
    for chunk in range(chunks):
        for copy in fetch(chunk):
            copy.wait()
        if chunk + AHEAD < chunks:
            for copy in fetch(chunk + AHEAD):
                copy.start()
        for block in range(chunk * step // BLK, (chunk + 1) * step // BLK):
            at = block * BLK
            weights = (order * signs[block:block + 1, :]).astype(jnp.float32).astype(jnp.bfloat16)
            own, other = (buffer_ref[at:at + BLK, :] for buffer_ref in buffer_refs)
            values = own + both[:, block:block + 1] * other
            high = values.astype(jnp.bfloat16)
            low = (values - high.astype(jnp.float32)).astype(jnp.bfloat16)
            mixed = jnp.dot(
                jnp.concatenate([weights, weights], axis=1),
                jnp.concatenate([high, low], axis=0),
                preferred_element_type=jnp.float32,
            )
            for half in range(2):
                table_ref[pl.ds(2 * at + half, BLK, stride=2), :] = mixed[:, half * cols:(half + 1) * cols]


def join_kernel(*refs):
    *list_refs, out_ref = refs
    for at, list_ref in enumerate(list_refs):
        rows = list_ref.shape[0]
        out_ref[at * rows:(at + 1) * rows, :] = list_ref[...]


def specs(smem, vmem):
    return [pl.BlockSpec(memory_space=pltpu.SMEM)] * smem + [pl.BlockSpec(memory_space=pltpu.VMEM)] * vmem


def floats(*shape):
    return jax.ShapeDtypeStruct(shape, jnp.float32)


def transform(full, me, matrix, signs, other_matrix, other_signs):
    rows, width = matrix.shape
    chunks = 4
    return pl.pallas_call(
        functools.partial(transform_kernel, full, chunks),
        in_specs=specs(1, 2) + [pl.BlockSpec(memory_space=pl.ANY)] * 2,
        out_specs=specs(0, 1)[0],
        out_shape=floats(2 * rows, width // 2),
        scratch_shapes=[pltpu.VMEM((rows, width), jnp.float32)] * 2 + [pltpu.SemaphoreType.DMA((chunks, 2))],
        compiler_params=pltpu.CompilerParams(vmem_limit_bytes=WIDE),
        cost_estimate=pl.CostEstimate(
            flops=16 * rows * BLK * width, bytes_accessed=12 * rows * width, transcendentals=0
        ),
        name="transform",
    )(me, signs, other_signs, matrix, other_matrix)


def pick_rows(geometry, me, list_refs, table_ref, out_ref, row, pick, start, slots):
    stride, full, scale = geometry
    unroll = max(u for u in range(1, 33) if slots % u == 0)
    group = jnp.right_shift(me, full)
    sign = parity_sign(jnp.bitwise_and(jnp.bitwise_xor(group, pick), group)).astype(jnp.float32) * scale
    list_ref = list_refs[pick % 4]
    base = pick // 4 * stride
    live = jnp.clip(list_ref[base + stride - BLK] - start, 0, slots)

    def body(step, carry):
        first = step * unroll
        for u in range(unroll):
            out_ref[row + first + u] = table_ref[list_ref[base + start + first + u]] * sign
        return carry

    lax.fori_loop(0, pl.cdiv(live, unroll), body, 0)


def distances(x, y):
    return [x | y << 1 | a << 2 | b << 3 for a in range(2) for b in range(2)]


def gather(geometry, parts, me_ref, *refs):
    list_refs, table_ref, out_refs = refs[:4], refs[4], refs[-len(parts):]
    for (start, slots, picks), out_ref in zip(parts, out_refs):
        for at, pick in enumerate(picks):
            pick_rows(geometry, me_ref[0], list_refs, table_ref, out_ref, at * slots, pick, start, slots)


def call(kernel, name, scalars, arrays, outs, after=(), scratch=(), flops=0):
    moved = 4 * sum(x.size for x in arrays) + 4 * sum(x.size for x in outs)
    return pl.pallas_call(
        kernel,
        in_specs=specs(len(scalars), len(arrays)) + [pl.BlockSpec(memory_space=pl.ANY)] * len(after),
        out_specs=specs(0, len(outs)),
        out_shape=list(outs),
        scratch_shapes=list(scratch),
        compiler_params=pltpu.CompilerParams(vmem_limit_bytes=GRANT),
        cost_estimate=pl.CostEstimate(flops=flops, bytes_accessed=moved, transcendentals=0),
        name=name,
    )(*scalars, *arrays, *after)


def gram_kernel(ry_ref, live_ref, *refs):
    *part_refs, sketch_ref, on_ref, mine_ref, next_ref, rows_ref, blocks_ref = refs
    slots, cols = rows_ref.shape[0] // 2, rows_ref.shape[1]
    start = 0
    for near_ref, add_ref in zip(part_refs[::2], part_refs[1::2]):
        rows_ref[start:start + near_ref.shape[0], :] = near_ref[...] + add_ref[...]
        start += near_ref.shape[0]
    values = jnp.concatenate([rows_ref[pl.ds(half, slots, stride=2), :] for half in range(2)], axis=1)
    live = lax.broadcasted_iota(jnp.int32, values.shape, 0) < live_ref[0]
    values = jnp.where(live, values, 0.0)
    sketch_ref[...] = values
    high = values.astype(jnp.bfloat16)
    low = (values - high.astype(jnp.float32)).astype(jnp.bfloat16)
    total = lax.dot_general(
        jnp.concatenate([high, high, low], axis=0),
        jnp.concatenate([high, low, high], axis=0),
        (((0,), (0,)), ((), ())),
        preferred_element_type=jnp.float32,
    )
    for block in range(4):
        a, b = block // 2, block % 2
        blocks_ref[block] = total[a * cols:(a + 1) * cols, b * cols:(b + 1) * cols]
    ry = ry_ref[0]
    mine_ref[...] = blocks_ref[ry]
    on_ref[:cols, :] = blocks_ref[jnp.bitwise_xor(ry, 1)]
    next_ref[...] = blocks_ref[jnp.bitwise_xor(ry, 2)]
    on_ref[cols:, :] = blocks_ref[jnp.bitwise_xor(ry, 3)]


def local(matrix, signs, indices, counts):
    rows, width = matrix.shape
    slots = indices.shape[0]
    cols = width // 2
    tail = slots // 32 * 9
    head = slots - tail
    first = head // 2
    size_x = lax.axis_size("rx")
    size_y = lax.axis_size("ry")
    size = size_x * size_y
    full = size.bit_length() - 1 - REST
    assert full >= 1 and size_y == 4
    ry = lax.axis_index("ry")
    me = lax.axis_index("rx") * size_y + ry
    scale = 1.0 / (size * BLK) ** 0.5
    stride = slots + BLK

    me_one = me.astype(jnp.int32).reshape(1)
    signs = signs.reshape(rows // BLK, BLK)
    if full > 1:
        matrix = (matrix.reshape(rows // BLK, BLK, width) * signs[:, :, None].astype(jnp.float32)).reshape(rows, width)
        signs = jnp.ones_like(signs)
    for bit in range(full - 1):
        other = swap(matrix, 1 << bit)
        matrix = jnp.where(jnp.bitwise_and(jnp.right_shift(me, bit), 1) == 1, other - matrix, matrix + other)
    own = jnp.concatenate([indices, jnp.pad(counts, (0, BLK - 1)), signs.reshape(-1)]).reshape(-1, BLK)
    own = lax.optimization_barrier(own)
    own_list = own[:stride // BLK]
    last = 1 << (full - 1)
    table = transform(full, me_one, matrix, own, swap(matrix, last), swap(own, last)).reshape(rows, 2, cols)
    column_lists = [own_list] + [swap(own_list, step << full) for step in (4, 8, 12)]
    (joined,) = call(
        join_kernel, "join", (), column_lists, (jax.ShapeDtypeStruct((4 * stride // BLK, BLK), jnp.int32),)
    )
    lists = [joined.reshape(-1)] + [swap(joined, step << full).reshape(-1) for step in (1, 2, 3)]

    geometry = (stride, full, scale)
    scalars = (me_one, *lists)

    def gathered(name, parts, after=()):
        outs = [floats(slots * len(picks), 2, cols) for _, slots, picks in parts]
        kernel = functools.partial(gather, geometry, parts)
        return [x.reshape(-1, cols) for x in call(kernel, name, scalars, (table,), outs, after=after)]

    a, b = (0, first), (first, head - first)
    *fars, end_on = gathered(
        "gather_far",
        [
            (*a, distances(1, 0) + distances(1, 1)),
            (*b, distances(0, 1) + distances(1, 1)),
            (head, tail, [z + near for z in (4, 12) for near in (0, 2, 1, 3)]),
        ],
    )
    end_add = swap(end_on, 4 << full)
    ends = gathered("gather_end", [(head, tail, [z + near for near in (0, 2, 1, 3)]) for z in (0, 8)])
    nears = gathered(
        "gather_near",
        [
            (*a, distances(0, 0)),
            (*a, distances(0, 1)),
            (*b, distances(0, 0)),
            (*b, distances(1, 0)),
        ],
        after=(end_on,),
    )

    def halved(value):
        middle = value.shape[0] // 2
        return value[:middle], value[middle:]

    for bits in (8, 1, 2):
        end, end_on = (own + add for own, add in zip(ends, halved(end_add)))
        end_add = swap(end_on, bits << full)
        ends = halved(end)

    finals = []
    for stays, far, steps in ((nears[:2], fars[0], (1, 2, 4, 8)), (nears[2:], fars[1], (2, 1, 4, 8))):
        for step in steps[:-1]:
            near, far = (own + add for own, add in zip(stays, halved(swap(far, step << full))))
            stays = halved(near)
        finals += [near, swap(far, steps[-1] << full)]

    sketch, on, block, far_block = call(
        gram_kernel,
        "gram",
        (ry.astype(jnp.int32).reshape(1), counts),
        (*finals, end, end_add),
        (floats(slots, width), floats(2 * cols, cols), floats(cols, cols), floats(cols, cols)),
        scratch=[pltpu.VMEM((2 * slots, cols), jnp.float32), pltpu.VMEM((4, cols, cols), jnp.float32)],
        flops=6 * slots * width * width,
    )
    got = swap(on, 1)
    block, far_block = block + got[:cols], far_block + got[cols:]
    block = block + swap(far_block, 2) + swap(block, size_y) + swap(far_block, 2 + size_y)
    at, bits = 1, size_x.bit_length() - 1
    while at < bits:
        together = min(2, bits - at)
        block = sum([swap(block, size_y * (step << at)) for step in range(1, 2**together)], block)
        at += together
    return sketch, (block * (1.0 / (size * slots)))[None]


def solution(mesh):
    in_specs = (P(("rx", "ry"), None), P(("rx", "ry")), P(("rx", "ry")), P(("rx", "ry")))
    out_specs = (P(("rx", "ry"), None), P("ry", None, None))
    return jax.shard_map(local, mesh=mesh, in_specs=in_specs, out_specs=out_specs, check_vma=False)
```

```python
import functools

import jax
import jax.numpy as jnp
from jax import lax
from jax.experimental import pallas as pl
from jax.experimental.pallas import tpu as pltpu
from jax.sharding import PartitionSpec as P

BLK = 128
MESH_AXES = ("rx", "ry")
GRANT = 12 * 2**20
WIDE = 46 * 2**20
AHEAD = 2
REST = 4


def swap(value, bits):
    size = lax.axis_size("rx") * lax.axis_size("ry")
    return lax.ppermute(value, MESH_AXES, [(i, i ^ bits) for i in range(size)])


def parity_sign(both):
    for shift in (4, 2, 1):
        both = jnp.bitwise_xor(both, jnp.right_shift(both, shift))
    return 1 - 2 * jnp.bitwise_and(both, 1)


def transform_kernel(full, chunks, me_ref, signs_ref, other_signs_ref, *refs):
    matrix_refs, table_ref, buffer_refs, sems = refs[:2], refs[2], refs[3:5], refs[5]
    rows, cols = table_ref.shape[0] // 2, table_ref.shape[1]
    step = rows // chunks

    def fetch(chunk):
        at = pl.ds(chunk * step, step)
        return [
            pltpu.make_async_copy(matrix_ref.at[at, :], buffer_ref.at[at, :], sems.at[chunk, which])
            for which, (matrix_ref, buffer_ref) in enumerate(zip(matrix_refs, buffer_refs))
        ]

    for chunk in range(AHEAD):
        for copy in fetch(chunk):
            copy.start()
    down = lax.broadcasted_iota(jnp.int32, (BLK, BLK), 0)
    across = lax.broadcasted_iota(jnp.int32, (BLK, BLK), 1)
    order = parity_sign(jnp.bitwise_and(down, across))
    upper = jnp.bitwise_and(jnp.right_shift(me_ref[0], full - 1), 1)
    last = signs_ref.shape[0] - rows // BLK
    signs = signs_ref[last:, :] * (1 - 2 * upper)
    both = (signs * other_signs_ref[last:, :]).astype(jnp.float32).T
    for chunk in range(chunks):
        for copy in fetch(chunk):
            copy.wait()
        if chunk + AHEAD < chunks:
            for copy in fetch(chunk + AHEAD):
                copy.start()
        for block in range(chunk * step // BLK, (chunk + 1) * step // BLK):
            at = block * BLK
            weights = (order * signs[block:block + 1, :]).astype(jnp.float32).astype(jnp.bfloat16)
            own, other = (buffer_ref[at:at + BLK, :] for buffer_ref in buffer_refs)
            values = own + both[:, block:block + 1] * other
            high = values.astype(jnp.bfloat16)
            low = (values - high.astype(jnp.float32)).astype(jnp.bfloat16)
            mixed = jnp.dot(
                jnp.concatenate([weights, weights], axis=1),
                jnp.concatenate([high, low], axis=0),
                preferred_element_type=jnp.float32,
            )
            for half in range(2):
                table_ref[pl.ds(2 * at + half, BLK, stride=2), :] = mixed[:, half * cols:(half + 1) * cols]


def join_kernel(*refs):
    *list_refs, out_ref = refs
    for at, list_ref in enumerate(list_refs):
        rows = list_ref.shape[0]
        out_ref[at * rows:(at + 1) * rows, :] = list_ref[...]


def specs(smem, vmem):
    return [pl.BlockSpec(memory_space=pltpu.SMEM)] * smem + [pl.BlockSpec(memory_space=pltpu.VMEM)] * vmem


def floats(*shape):
    return jax.ShapeDtypeStruct(shape, jnp.float32)


def transform(full, me, matrix, signs, other_matrix, other_signs):
    rows, width = matrix.shape
    chunks = 4
    return pl.pallas_call(
        functools.partial(transform_kernel, full, chunks),
        in_specs=specs(1, 2) + [pl.BlockSpec(memory_space=pl.ANY)] * 2,
        out_specs=specs(0, 1)[0],
        out_shape=floats(2 * rows, width // 2),
        scratch_shapes=[pltpu.VMEM((rows, width), jnp.float32)] * 2 + [pltpu.SemaphoreType.DMA((chunks, 2))],
        compiler_params=pltpu.CompilerParams(vmem_limit_bytes=WIDE),
        cost_estimate=pl.CostEstimate(
            flops=16 * rows * BLK * width, bytes_accessed=12 * rows * width, transcendentals=0
        ),
        name="transform",
    )(me, signs, other_signs, matrix, other_matrix)


def pick_rows(geometry, me, list_refs, table_ref, out_ref, row, pick, start, slots):
    stride, full, scale = geometry
    unroll = max(u for u in range(1, 33) if slots % u == 0)
    group = jnp.right_shift(me, full)
    sign = parity_sign(jnp.bitwise_and(jnp.bitwise_xor(group, pick), group)).astype(jnp.float32) * scale
    list_ref = list_refs[pick % 4]
    base = pick // 4 * stride
    live = jnp.clip(list_ref[base + stride - BLK] - start, 0, slots)

    def body(step, carry):
        first = step * unroll
        for u in range(unroll):
            out_ref[row + first + u] = table_ref[list_ref[base + start + first + u]] * sign
        return carry

    lax.fori_loop(0, pl.cdiv(live, unroll), body, 0)


def distances(x, y):
    return [x | y << 1 | a << 2 | b << 3 for a in range(2) for b in range(2)]


def gather(geometry, parts, me_ref, *refs):
    list_refs, table_ref, out_refs = refs[:4], refs[4], refs[-len(parts):]
    for (start, slots, picks), out_ref in zip(parts, out_refs):
        for at, pick in enumerate(picks):
            pick_rows(geometry, me_ref[0], list_refs, table_ref, out_ref, at * slots, pick, start, slots)


def call(kernel, name, scalars, arrays, outs, after=(), scratch=(), flops=0):
    moved = 4 * sum(x.size for x in arrays) + 4 * sum(x.size for x in outs)
    return pl.pallas_call(
        kernel,
        in_specs=specs(len(scalars), len(arrays)) + [pl.BlockSpec(memory_space=pl.ANY)] * len(after),
        out_specs=specs(0, len(outs)),
        out_shape=list(outs),
        scratch_shapes=list(scratch),
        compiler_params=pltpu.CompilerParams(vmem_limit_bytes=GRANT),
        cost_estimate=pl.CostEstimate(flops=flops, bytes_accessed=moved, transcendentals=0),
        name=name,
    )(*scalars, *arrays, *after)


def gram_kernel(ry_ref, live_ref, *refs):
    *part_refs, sketch_ref, on_ref, mine_ref, next_ref, rows_ref, blocks_ref = refs
    slots, cols = rows_ref.shape[0] // 2, rows_ref.shape[1]
    start = 0
    for near_ref, add_ref in zip(part_refs[::2], part_refs[1::2]):
        rows_ref[start:start + near_ref.shape[0], :] = near_ref[...] + add_ref[...]
        start += near_ref.shape[0]
    values = jnp.concatenate([rows_ref[pl.ds(half, slots, stride=2), :] for half in range(2)], axis=1)
    live = lax.broadcasted_iota(jnp.int32, values.shape, 0) < live_ref[0]
    values = jnp.where(live, values, 0.0)
    sketch_ref[...] = values
    high = values.astype(jnp.bfloat16)
    low = (values - high.astype(jnp.float32)).astype(jnp.bfloat16)
    total = lax.dot_general(
        jnp.concatenate([high, high, low], axis=0),
        jnp.concatenate([high, low, high], axis=0),
        (((0,), (0,)), ((), ())),
        preferred_element_type=jnp.float32,
    )
    for block in range(4):
        a, b = block // 2, block % 2
        blocks_ref[block] = total[a * cols:(a + 1) * cols, b * cols:(b + 1) * cols]
    ry = ry_ref[0]
    mine_ref[...] = blocks_ref[ry]
    on_ref[:cols, :] = blocks_ref[jnp.bitwise_xor(ry, 1)]
    next_ref[...] = blocks_ref[jnp.bitwise_xor(ry, 2)]
    on_ref[cols:, :] = blocks_ref[jnp.bitwise_xor(ry, 3)]


def local(matrix, signs, indices, counts):
    rows, width = matrix.shape
    slots = indices.shape[0]
    cols = width // 2
    tail = slots // 4
    head = slots - tail
    first = head // 2
    size_x = lax.axis_size("rx")
    size_y = lax.axis_size("ry")
    size = size_x * size_y
    full = size.bit_length() - 1 - REST
    assert full >= 1 and size_y == 4
    ry = lax.axis_index("ry")
    me = lax.axis_index("rx") * size_y + ry
    scale = 1.0 / (size * BLK) ** 0.5
    stride = slots + BLK

    me_one = me.astype(jnp.int32).reshape(1)
    signs = signs.reshape(rows // BLK, BLK)
    if full > 1:
        matrix = (matrix.reshape(rows // BLK, BLK, width) * signs[:, :, None].astype(jnp.float32)).reshape(rows, width)
        signs = jnp.ones_like(signs)
    for bit in range(full - 1):
        other = swap(matrix, 1 << bit)
        matrix = jnp.where(jnp.bitwise_and(jnp.right_shift(me, bit), 1) == 1, other - matrix, matrix + other)
    own = jnp.concatenate([indices, jnp.pad(counts, (0, BLK - 1)), signs.reshape(-1)]).reshape(-1, BLK)
    own = lax.optimization_barrier(own)
    own_list = own[:stride // BLK]
    last = 1 << (full - 1)
    table = transform(full, me_one, matrix, own, swap(matrix, last), swap(own, last)).reshape(rows, 2, cols)
    column_lists = [own_list] + [swap(own_list, step << full) for step in (4, 8, 12)]
    (joined,) = call(
        join_kernel, "join", (), column_lists, (jax.ShapeDtypeStruct((4 * stride // BLK, BLK), jnp.int32),)
    )
    lists = [joined.reshape(-1)] + [swap(joined, step << full).reshape(-1) for step in (1, 2, 3)]

    geometry = (stride, full, scale)
    scalars = (me_one, *lists)

    def gathered(name, parts, after=()):
        outs = [floats(slots * len(picks), 2, cols) for _, slots, picks in parts]
        kernel = functools.partial(gather, geometry, parts)
        return [x.reshape(-1, cols) for x in call(kernel, name, scalars, (table,), outs, after=after)]

    a, b = (0, first), (first, head - first)
    *fars, end_on = gathered(
        "gather_far",
        [
            (*a, distances(1, 0) + distances(1, 1)),
            (*b, distances(0, 1) + distances(1, 1)),
            (head, tail, [z + near for z in (4, 12) for near in (0, 2, 1, 3)]),
        ],
    )
    end_add = swap(end_on, 4 << full)
    ends = gathered("gather_end", [(head, tail, [z + near for near in (0, 2, 1, 3)]) for z in (0, 8)])
    nears = gathered(
        "gather_near",
        [
            (*a, distances(0, 0)),
            (*a, distances(0, 1)),
            (*b, distances(0, 0)),
            (*b, distances(1, 0)),
        ],
        after=(end_on,),
    )

    def halved(value):
        middle = value.shape[0] // 2
        return value[:middle], value[middle:]

    for bits in (8, 1, 2):
        end, end_on = (own + add for own, add in zip(ends, halved(end_add)))
        end_add = swap(end_on, bits << full)
        ends = halved(end)

    finals = []
    for stays, far, steps in ((nears[:2], fars[0], (1, 2, 4, 8)), (nears[2:], fars[1], (2, 1, 4, 8))):
        for step in steps[:-1]:
            near, far = (own + add for own, add in zip(stays, halved(swap(far, step << full))))
            stays = halved(near)
        finals += [near, swap(far, steps[-1] << full)]

    sketch, on, block, far_block = call(
        gram_kernel,
        "gram",
        (ry.astype(jnp.int32).reshape(1), counts),
        (*finals, end, end_add),
        (floats(slots, width), floats(2 * cols, cols), floats(cols, cols), floats(cols, cols)),
        scratch=[pltpu.VMEM((2 * slots, cols), jnp.float32), pltpu.VMEM((4, cols, cols), jnp.float32)],
        flops=6 * slots * width * width,
    )
    got = swap(on, 1)
    block, far_block = block + got[:cols], far_block + got[cols:]
    block = block + swap(far_block, 2) + swap(block, size_y) + swap(far_block, 2 + size_y)
    at, bits = 1, size_x.bit_length() - 1
    while at < bits:
        together = min(2, bits - at)
        block = sum([swap(block, size_y * (step << at)) for step in range(1, 2**together)], block)
        at += together
    return sketch, (block * (1.0 / (size * slots)))[None]


def solution(mesh):
    in_specs = (P(("rx", "ry"), None), P(("rx", "ry")), P(("rx", "ry")), P(("rx", "ry")))
    out_specs = (P(("rx", "ry"), None), P("ry", None, None))
    return jax.shard_map(local, mesh=mesh, in_specs=in_specs, out_specs=out_specs, check_vma=False)
```

```python
import functools

import jax
import jax.numpy as jnp
from jax import lax
from jax.experimental import pallas as pl
from jax.experimental.pallas import tpu as pltpu
from jax.sharding import PartitionSpec as P

BLK = 128
MESH_AXES = ("rx", "ry")
GRANT = 12 * 2**20
WIDE = 46 * 2**20
AHEAD = 4
REST = 4


def swap(value, bits):
    size = lax.axis_size("rx") * lax.axis_size("ry")
    return lax.ppermute(value, MESH_AXES, [(i, i ^ bits) for i in range(size)])


def parity_sign(both):
    for shift in (4, 2, 1):
        both = jnp.bitwise_xor(both, jnp.right_shift(both, shift))
    return 1 - 2 * jnp.bitwise_and(both, 1)


def transform_kernel(full, chunks, me_ref, signs_ref, other_signs_ref, *refs):
    matrix_refs, table_ref, buffer_refs, sems = refs[:2], refs[2], refs[3:5], refs[5]
    rows, cols = table_ref.shape[0] // 2, table_ref.shape[1]
    step = rows // chunks

    def fetch(chunk):
        at = pl.ds(chunk * step, step)
        return [
            pltpu.make_async_copy(matrix_ref.at[at, :], buffer_ref.at[at, :], sems.at[chunk, which])
            for which, (matrix_ref, buffer_ref) in enumerate(zip(matrix_refs, buffer_refs))
        ]

    for chunk in range(AHEAD):
        for copy in fetch(chunk):
            copy.start()
    down = lax.broadcasted_iota(jnp.int32, (BLK, BLK), 0)
    across = lax.broadcasted_iota(jnp.int32, (BLK, BLK), 1)
    order = parity_sign(jnp.bitwise_and(down, across))
    upper = jnp.bitwise_and(jnp.right_shift(me_ref[0], full - 1), 1)
    last = signs_ref.shape[0] - rows // BLK
    signs = signs_ref[last:, :] * (1 - 2 * upper)
    both = (signs * other_signs_ref[last:, :]).astype(jnp.float32).T
    for chunk in range(chunks):
        for copy in fetch(chunk):
            copy.wait()
        if chunk + AHEAD < chunks:
            for copy in fetch(chunk + AHEAD):
                copy.start()
        for block in range(chunk * step // BLK, (chunk + 1) * step // BLK):
            at = block * BLK
            weights = (order * signs[block:block + 1, :]).astype(jnp.float32).astype(jnp.bfloat16)
            own, other = (buffer_ref[at:at + BLK, :] for buffer_ref in buffer_refs)
            values = own + both[:, block:block + 1] * other
            high = values.astype(jnp.bfloat16)
            low = (values - high.astype(jnp.float32)).astype(jnp.bfloat16)
            mixed = jnp.dot(
                jnp.concatenate([weights, weights], axis=1),
                jnp.concatenate([high, low], axis=0),
                preferred_element_type=jnp.float32,
            )
            for half in range(2):
                table_ref[pl.ds(2 * at + half, BLK, stride=2), :] = mixed[:, half * cols:(half + 1) * cols]


def join_kernel(*refs):
    *list_refs, out_ref = refs
    for at, list_ref in enumerate(list_refs):
        rows = list_ref.shape[0]
        out_ref[at * rows:(at + 1) * rows, :] = list_ref[...]


def specs(smem, vmem):
    return [pl.BlockSpec(memory_space=pltpu.SMEM)] * smem + [pl.BlockSpec(memory_space=pltpu.VMEM)] * vmem


def floats(*shape):
    return jax.ShapeDtypeStruct(shape, jnp.float32)


def transform(full, me, matrix, signs, other_matrix, other_signs):
    rows, width = matrix.shape
    chunks = 4
    return pl.pallas_call(
        functools.partial(transform_kernel, full, chunks),
        in_specs=specs(1, 2) + [pl.BlockSpec(memory_space=pl.ANY)] * 2,
        out_specs=specs(0, 1)[0],
        out_shape=floats(2 * rows, width // 2),
        scratch_shapes=[pltpu.VMEM((rows, width), jnp.float32)] * 2 + [pltpu.SemaphoreType.DMA((chunks, 2))],
        compiler_params=pltpu.CompilerParams(vmem_limit_bytes=WIDE),
        cost_estimate=pl.CostEstimate(
            flops=16 * rows * BLK * width, bytes_accessed=12 * rows * width, transcendentals=0
        ),
        name="transform",
    )(me, signs, other_signs, matrix, other_matrix)


def pick_rows(geometry, me, list_refs, table_ref, out_ref, row, pick, start, slots):
    stride, full, scale = geometry
    unroll = max(u for u in range(1, 33) if slots % u == 0)
    group = jnp.right_shift(me, full)
    sign = parity_sign(jnp.bitwise_and(jnp.bitwise_xor(group, pick), group)).astype(jnp.float32) * scale
    list_ref = list_refs[pick % 4]
    base = pick // 4 * stride
    live = jnp.clip(list_ref[base + stride - BLK] - start, 0, slots)

    def body(step, carry):
        first = step * unroll
        for u in range(unroll):
            out_ref[row + first + u] = table_ref[list_ref[base + start + first + u]] * sign
        return carry

    lax.fori_loop(0, pl.cdiv(live, unroll), body, 0)


def distances(x, y):
    return [x | y << 1 | a << 2 | b << 3 for a in range(2) for b in range(2)]


def gather(geometry, parts, me_ref, *refs):
    list_refs, table_ref, out_refs = refs[:4], refs[4], refs[-len(parts):]
    for (start, slots, picks), out_ref in zip(parts, out_refs):
        for at, pick in enumerate(picks):
            pick_rows(geometry, me_ref[0], list_refs, table_ref, out_ref, at * slots, pick, start, slots)


def call(kernel, name, scalars, arrays, outs, after=(), scratch=(), flops=0):
    moved = 4 * sum(x.size for x in arrays) + 4 * sum(x.size for x in outs)
    return pl.pallas_call(
        kernel,
        in_specs=specs(len(scalars), len(arrays)) + [pl.BlockSpec(memory_space=pl.ANY)] * len(after),
        out_specs=specs(0, len(outs)),
        out_shape=list(outs),
        scratch_shapes=list(scratch),
        compiler_params=pltpu.CompilerParams(vmem_limit_bytes=GRANT),
        cost_estimate=pl.CostEstimate(flops=flops, bytes_accessed=moved, transcendentals=0),
        name=name,
    )(*scalars, *arrays, *after)


def gram_kernel(ry_ref, live_ref, *refs):
    *part_refs, sketch_ref, on_ref, mine_ref, next_ref, rows_ref, blocks_ref = refs
    slots, cols = rows_ref.shape[0] // 2, rows_ref.shape[1]
    start = 0
    for near_ref, add_ref in zip(part_refs[::2], part_refs[1::2]):
        rows_ref[start:start + near_ref.shape[0], :] = near_ref[...] + add_ref[...]
        start += near_ref.shape[0]
    values = jnp.concatenate([rows_ref[pl.ds(half, slots, stride=2), :] for half in range(2)], axis=1)
    live = lax.broadcasted_iota(jnp.int32, values.shape, 0) < live_ref[0]
    values = jnp.where(live, values, 0.0)
    sketch_ref[...] = values
    high = values.astype(jnp.bfloat16)
    low = (values - high.astype(jnp.float32)).astype(jnp.bfloat16)
    total = lax.dot_general(
        jnp.concatenate([high, high, low], axis=0),
        jnp.concatenate([high, low, high], axis=0),
        (((0,), (0,)), ((), ())),
        preferred_element_type=jnp.float32,
    )
    for block in range(4):
        a, b = block // 2, block % 2
        blocks_ref[block] = total[a * cols:(a + 1) * cols, b * cols:(b + 1) * cols]
    ry = ry_ref[0]
    mine_ref[...] = blocks_ref[ry]
    on_ref[:cols, :] = blocks_ref[jnp.bitwise_xor(ry, 1)]
    next_ref[...] = blocks_ref[jnp.bitwise_xor(ry, 2)]
    on_ref[cols:, :] = blocks_ref[jnp.bitwise_xor(ry, 3)]


def local(matrix, signs, indices, counts):
    rows, width = matrix.shape
    slots = indices.shape[0]
    cols = width // 2
    tail = slots // 4
    head = slots - tail
    first = head // 2
    size_x = lax.axis_size("rx")
    size_y = lax.axis_size("ry")
    size = size_x * size_y
    full = size.bit_length() - 1 - REST
    assert full >= 1 and size_y == 4
    ry = lax.axis_index("ry")
    me = lax.axis_index("rx") * size_y + ry
    scale = 1.0 / (size * BLK) ** 0.5
    stride = slots + BLK

    me_one = me.astype(jnp.int32).reshape(1)
    signs = signs.reshape(rows // BLK, BLK)
    if full > 1:
        matrix = (matrix.reshape(rows // BLK, BLK, width) * signs[:, :, None].astype(jnp.float32)).reshape(rows, width)
        signs = jnp.ones_like(signs)
    for bit in range(full - 1):
        other = swap(matrix, 1 << bit)
        matrix = jnp.where(jnp.bitwise_and(jnp.right_shift(me, bit), 1) == 1, other - matrix, matrix + other)
    own = jnp.concatenate([indices, jnp.pad(counts, (0, BLK - 1)), signs.reshape(-1)]).reshape(-1, BLK)
    own = lax.optimization_barrier(own)
    own_list = own[:stride // BLK]
    last = 1 << (full - 1)
    table = transform(full, me_one, matrix, own, swap(matrix, last), swap(own, last)).reshape(rows, 2, cols)
    column_lists = [own_list] + [swap(own_list, step << full) for step in (4, 8, 12)]
    (joined,) = call(
        join_kernel, "join", (), column_lists, (jax.ShapeDtypeStruct((4 * stride // BLK, BLK), jnp.int32),)
    )
    lists = [joined.reshape(-1)] + [swap(joined, step << full).reshape(-1) for step in (1, 2, 3)]

    geometry = (stride, full, scale)
    scalars = (me_one, *lists)

    def gathered(name, parts, after=()):
        outs = [floats(slots * len(picks), 2, cols) for _, slots, picks in parts]
        kernel = functools.partial(gather, geometry, parts)
        return [x.reshape(-1, cols) for x in call(kernel, name, scalars, (table,), outs, after=after)]

    a, b = (0, first), (first, head - first)
    *fars, end_on = gathered(
        "gather_far",
        [
            (*a, distances(1, 0) + distances(1, 1)),
            (*b, distances(0, 1) + distances(1, 1)),
            (head, tail, [z + near for z in (4, 12) for near in (0, 2, 1, 3)]),
        ],
    )
    end_add = swap(end_on, 4 << full)
    ends = gathered("gather_end", [(head, tail, [z + near for near in (0, 2, 1, 3)]) for z in (0, 8)])
    nears = gathered(
        "gather_near",
        [
            (*a, distances(0, 0)),
            (*a, distances(0, 1)),
            (*b, distances(0, 0)),
            (*b, distances(1, 0)),
        ],
        after=(end_on,),
    )

    def halved(value):
        middle = value.shape[0] // 2
        return value[:middle], value[middle:]

    for bits in (8, 1, 2):
        end, end_on = (own + add for own, add in zip(ends, halved(end_add)))
        end_add = swap(end_on, bits << full)
        ends = halved(end)

    finals = []
    for stays, far, steps in ((nears[:2], fars[0], (1, 2, 4, 8)), (nears[2:], fars[1], (2, 1, 4, 8))):
        for step in steps[:-1]:
            near, far = (own + add for own, add in zip(stays, halved(swap(far, step << full))))
            stays = halved(near)
        finals += [near, swap(far, steps[-1] << full)]

    sketch, on, block, far_block = call(
        gram_kernel,
        "gram",
        (ry.astype(jnp.int32).reshape(1), counts),
        (*finals, end, end_add),
        (floats(slots, width), floats(2 * cols, cols), floats(cols, cols), floats(cols, cols)),
        scratch=[pltpu.VMEM((2 * slots, cols), jnp.float32), pltpu.VMEM((4, cols, cols), jnp.float32)],
        flops=6 * slots * width * width,
    )
    got = swap(on, 1)
    block, far_block = block + got[:cols], far_block + got[cols:]
    block = block + swap(far_block, 2) + swap(block, size_y) + swap(far_block, 2 + size_y)
    at, bits = 1, size_x.bit_length() - 1
    while at < bits:
        together = min(2, bits - at)
        block = sum([swap(block, size_y * (step << at)) for step in range(1, 2**together)], block)
        at += together
    return sketch, (block * (1.0 / (size * slots)))[None]


def solution(mesh):
    in_specs = (P(("rx", "ry"), None), P(("rx", "ry")), P(("rx", "ry")), P(("rx", "ry")))
    out_specs = (P(("rx", "ry"), None), P("ry", None, None))
    return jax.shard_map(local, mesh=mesh, in_specs=in_specs, out_specs=out_specs, check_vma=False)
```
